32 devices in a mesh: lines: 2 (over y), strip: 8 (over z, x), wave: 2 (over core).
Axes of the slice: x: 2, y: 2, z: 4, core: 2. Of those that a mesh axis runs over, the one named last changes fastest.
Arguments:
- prior_fields: float32 [12, 2, 128, 2048], P('wave', None, ('lines', 'strip')), parts along dimension 2, may hold values from -4 to 4
- conductivity: float32 [128, 2048], P(('lines', 'strip')), parts along dimension 0, may hold values from 0.2 to 5
- electrode_nodes: int32 [128], P('lines'), parts along dimension 0, may hold values from 0 to 131071, as said below
- source_pair: int32 [4], P('lines'), parts along dimension 0, may hold values from 0 to 63
- innovation: float32 [128], P('lines'), parts along dimension 0, may hold values from -6 to 6
Outputs:
- gradient: float32 [128, 2048], P(('lines', 'strip'), 'wave'), parts along dimension 0
The draws below stay inside these ranges and needn't reach their ends.
There are 2 independent parts, one for each index of `lines`. The reference program is written for one: setup_inputs(seed, part) draws one part's arguments, and reference() takes and returns one part's arrays. A program takes and returns all parts, laid end to end along the dimension named above; each array names one. Nothing has to cross between parts.
Inputs may be any that keep to these rules, and one draw needn't show every extreme that they name: `electrode_nodes`: nodes may repeat. `source_pair`: the two numbers may be equal.
All inputs are finite; a program needn't handle non-finite values.
Results may differ from the reference program's by a relative error of at most 0.0003.
Values sent between devices are 32-bit elements; how exact they have to be, the bound alone decides.
A program may use at most 64 MiB of HBM per device.

```python
import math
import jax
import jax.numpy as jnp
from jax import lax

WAVES = 12
NX = 2048
NE = 64
ITERS = 12
NZ = 64


k_lowest = 0.01


k_highest = 1.0


def electrode_draw(key):
    return jax.random.randint(jax.random.fold_in(key, 101), (NE,), 0, NZ * NX).astype(jnp.int32)


def profiles(offset, wavenum):
    distance = jnp.abs(offset).astype(jnp.float32)
    return jnp.exp(-wavenum[:, None] * distance[None, :]) / jnp.sqrt(1.0 + distance[None, :])


def draw_electrode_nodes(key, part):
    return electrode_draw(key)


def draw_prior_fields(key, part):
    nodes = electrode_draw(key)
    key = jax.random.fold_in(key, 7)
    pair_key, weight_key, noise_key = jax.random.split(key, 3)
    spacing = (math.log(k_highest) - math.log(k_lowest)) / (WAVES - 1)
    wavenum = jnp.exp(math.log(k_lowest) + spacing * jnp.arange(WAVES).astype(jnp.float32))
    node_rows = nodes // NX
    node_cols = nodes % NX
    row_axis = jnp.arange(NZ, dtype=jnp.int32)
    col_axis = jnp.arange(NX, dtype=jnp.int32)

    def kernel(index):
        depth_part = profiles(row_axis - node_rows[index], wavenum)
        lateral = profiles(col_axis - node_cols[index], wavenum)
        return depth_part[:, :, None] * lateral[:, None, :]
    pair = jax.random.randint(pair_key, (2,), 0, NE)
    amplitude = 1.0
    charges = jnp.clip(jax.random.normal(weight_key, (NE,), jnp.float32), -2.5, 2.5)
    noise = 0.01 * jnp.clip(jax.random.normal(noise_key, (WAVES, 2, NZ, NX), jnp.float32), -4.0, 4.0)
    forward = amplitude * (kernel(pair[0]) - kernel(pair[1]))

    def accumulate(index, total):
        return total + charges[index] * kernel(index)
    adjoint = amplitude * lax.fori_loop(0, NE, accumulate, jnp.zeros((WAVES, NZ, NX), jnp.float32))
    result = jnp.stack([forward, adjoint], axis=1) + noise
    return jnp.clip(result, -4.0, 4.0).astype(jnp.float32)


def shard_levels(key, dims, shards, least, high):
    level = 1.0
    for axis_at, shards_of in shards:
        heights = jax.random.uniform(jax.random.fold_in(jax.random.fold_in(key, 6), axis_at), (shards_of,), jnp.float32, least / len(shards), high / len(shards))
        level = level * jnp.repeat(jnp.exp(heights), dims[axis_at] // shards_of).reshape((-1,) + (1,) * (len(dims) - 1 - axis_at))
    return level


def bell_draw(own_key, dims, deviation, bound, kind=jnp.bfloat16):
    entries = deviation * jax.random.normal(own_key, dims, jnp.float32)
    return jnp.clip(entries, min=-bound, max=bound).astype(kind)


def setup_inputs(seed: int = 0, part: int = 0) -> dict:
    keys = jax.random.split(jax.random.key(seed), 6)
    part_splits = jax.random.split(jax.random.fold_in(keys[5], part), 6)
    prior_fields = draw_prior_fields(jax.random.fold_in(jax.random.fold_in(keys[5], part), 71), part)
    conductivity = jnp.clip(jnp.exp(math.log(5.0) - 3.218876 * jax.random.uniform(part_splits[1], (NZ, NX), jnp.float32) ** shard_levels(part_splits[1], (NZ, NX), ((0, 8),), -0.2, 0.2)), 0.2, 5.0)
    electrode_nodes = draw_electrode_nodes(jax.random.fold_in(jax.random.fold_in(keys[5], part), 71), part)
    source_pair = jax.random.randint(part_splits[3], (2,), 0, NE).astype(jnp.int32)
    innovation = bell_draw(part_splits[4], (NE,), 1.0, 6.0, jnp.float32)
    return {"prior_fields": prior_fields, "conductivity": conductivity, "electrode_nodes": electrode_nodes, "source_pair": source_pair, "innovation": innovation}


k_lowest = 0.01
k_highest = 1.0


def wave_table(position):
    spacing = (math.log(k_highest) - math.log(k_lowest)) / (WAVES - 1)
    wavenum = jnp.exp(math.log(k_lowest) + spacing * position)
    ends = jnp.where((position == 0) | (position == WAVES - 1), 0.5, 1.0)
    weights = (2.0 / math.pi) * spacing * wavenum * ends
    return wavenum, weights


def face_values(conductivity):
    padded = jnp.pad(conductivity, 1)
    row_ids = jnp.arange(conductivity.shape[0])[:, None]
    face_up = 0.5 * (conductivity + padded[:-2, 1:-1])
    face_up = jnp.where(row_ids == 0, 0.0, face_up)
    face_down = 0.5 * (conductivity + padded[2:, 1:-1])
    face_left = 0.5 * (conductivity + padded[1:-1, :-2])
    face_right = 0.5 * (conductivity + padded[1:-1, 2:])
    return face_up, face_down, face_left, face_right


def operate(vector, diagonal, faces):
    face_up, face_down, face_left, face_right = faces
    padded = jnp.pad(vector, ((0, 0), (0, 0), (1, 1), (1, 1)))
    result = diagonal * vector - face_up * padded[:, :, :-2, 1:-1]
    result = result - face_down * padded[:, :, 2:, 1:-1]
    result = result - face_left * padded[:, :, 1:-1, :-2]
    return result - face_right * padded[:, :, 1:-1, 2:]


def reference(prior_fields, conductivity, electrode_nodes, source_pair, innovation):
    faces = face_values(conductivity)
    wavenum, weights = wave_table(jnp.arange(WAVES).astype(jnp.float32))
    face_sum = faces[0] + faces[1] + faces[2] + faces[3]
    diagonal = (face_sum[None] + (wavenum * wavenum)[:, None, None] * conductivity[None])[:, None]
    electrode_ids = jnp.arange(NE)
    forward = (electrode_ids == source_pair[0]).astype(jnp.float32) - (electrode_ids == source_pair[1]).astype(jnp.float32)
    values = jnp.stack([forward, innovation.astype(jnp.float32)])
    flat_source = jnp.zeros((2, NZ * NX), jnp.float32).at[:, electrode_nodes].add(values)
    source = flat_source.reshape(2, NZ, NX)[None]
    solution = prior_fields
    residual = source - operate(solution, diagonal, faces)
    direction = residual
    norm_now = jnp.sum(residual * residual, axis=(2, 3), keepdims=True)
    for sweep in range(ITERS):
        applied = operate(direction, diagonal, faces)
        curve = jnp.sum(direction * applied, axis=(2, 3), keepdims=True)
        step_size = norm_now / curve
        solution = solution + step_size * direction
        residual = residual - step_size * applied
        norm_next = jnp.sum(residual * residual, axis=(2, 3), keepdims=True)
        direction = residual + (norm_next / norm_now) * direction
        norm_now = norm_next
    forward_field = solution[:, 0]
    adjoint_field = solution[:, 1]
    fwd_pad = jnp.pad(forward_field, ((0, 0), (1, 1), (1, 1)))
    adj_pad = jnp.pad(adjoint_field, ((0, 0), (1, 1), (1, 1)))
    top_keep = (jnp.arange(NZ) != 0)[None, :, None]
    term_up = jnp.where(top_keep, (forward_field - fwd_pad[:, :-2, 1:-1]) * (adjoint_field - adj_pad[:, :-2, 1:-1]), 0.0)
    term_down = (forward_field - fwd_pad[:, 2:, 1:-1]) * (adjoint_field - adj_pad[:, 2:, 1:-1])
    term_left = (forward_field - fwd_pad[:, 1:-1, :-2]) * (adjoint_field - adj_pad[:, 1:-1, :-2])
    term_right = (forward_field - fwd_pad[:, 1:-1, 2:]) * (adjoint_field - adj_pad[:, 1:-1, 2:])
    partial_value = (wavenum * wavenum)[:, None, None] * forward_field * adjoint_field + 0.5 * (term_up + term_down + term_left + term_right)
    return -jnp.sum(weights[:, None, None] * partial_value, axis=0)
```

```python
import math

import jax
import jax.numpy as jnp
from jax import lax
from jax.experimental import pallas as pl
from jax.experimental.pallas import tpu as pltpu
from jax.sharding import PartitionSpec as P

WAVES = 12
ITERS = 12


k_lowest = 0.01
k_highest = 1.0


def padded_2(block, sides, width):
    for axis, dim in sides:
        count = lax.axis_size(axis)
        forward = [(i, i + 1) for i in range(count - 1)]
        backward = [(target, source) for source, target in forward]
        low = lax.ppermute(
            lax.slice_in_dim(block, block.shape[dim] - width, None, axis=dim), axis, forward
        )
        high = lax.ppermute(lax.slice_in_dim(block, 0, width, axis=dim), axis, backward)
        block = jnp.concatenate([low, block, high], axis=dim)
    return block


def wave_table(position):
    spacing = (math.log(k_highest) - math.log(k_lowest)) / (WAVES - 1)
    wavenum = jnp.exp(math.log(k_lowest) + spacing * position)
    ends = jnp.where((position == 0) | (position == WAVES - 1), 0.5, 1.0)
    weights = 2.0 / math.pi * spacing * wavenum * ends
    return (wavenum, weights)


def inner_sums(first, second):
    return jnp.sum(first * second, axis=(2, 3), keepdims=True)


def per_device_strips(prior_fields, conductivity, electrode_nodes, source_pair, innovation):
    wave_dev = prior_fields.shape[0]
    row_count = prior_fields.shape[2]
    cell_count = prior_fields.shape[3]
    row_ids = lax.axis_index("strip") * row_count + jnp.arange(row_count, dtype=jnp.int32)
    top_keep = (row_ids != 0)[:, None]
    sig_pad = padded_2(conductivity, (("strip", 0),), 1)
    sig_pad = jnp.pad(sig_pad, ((0, 0), (1, 1)))
    face_up = jnp.where(top_keep, 0.5 * (conductivity + sig_pad[:-2, 1:-1]), 0.0)
    face_down = 0.5 * (conductivity + sig_pad[2:, 1:-1])
    face_left = 0.5 * (conductivity + sig_pad[1:-1, :-2])
    face_right = 0.5 * (conductivity + sig_pad[1:-1, 2:])
    wave_ids = (lax.axis_index("wave") * wave_dev + jnp.arange(wave_dev, dtype=jnp.int32)).astype(
        jnp.float32
    )
    wavenum, weights = wave_table(wave_ids)
    face_sum = face_up + face_down + face_left + face_right
    diagonal = (face_sum[None] + (wavenum * wavenum)[:, None, None] * conductivity[None])[:, None]

    def operate(vector):
        padded = padded_2(vector, (("strip", 2),), 1)
        padded = jnp.pad(padded, ((0, 0), (0, 0), (0, 0), (1, 1)))
        result = diagonal * vector - face_up * padded[:, :, :-2, 1:-1]
        result = result - face_down * padded[:, :, 2:, 1:-1]
        result = result - face_left * padded[:, :, 1:-1, :-2]
        return result - face_right * padded[:, :, 1:-1, 2:]

    electrode_ids = jnp.arange(innovation.shape[0], dtype=jnp.int32)
    forward = (electrode_ids == source_pair[0]).astype(jnp.float32) - (
        electrode_ids == source_pair[1]
    ).astype(jnp.float32)
    values = jnp.stack([forward, innovation])
    node_rows = electrode_nodes // cell_count
    node_cols = electrode_nodes % cell_count
    rows_hot = (node_rows[:, None] == row_ids[None, :]).astype(jnp.float32)
    cols_hot = (node_cols[:, None] == jnp.arange(cell_count, dtype=jnp.int32)[None, :]).astype(
        jnp.float32
    )
    weighted = values[:, :, None] * rows_hot[None]
    source = jnp.einsum("sez,ex->szx", weighted, cols_hot, precision=lax.Precision.HIGHEST)[None]
    solution = prior_fields
    residual = source - operate(solution)

    def both_sums(vector, applied):
        return lax.psum((inner_sums(vector, vector), inner_sums(vector, applied)), "strip")

    applied = operate(residual)
    norm_now, product = both_sums(residual, applied)
    step_size = norm_now / product

    def iterate(sweep, carry):
        solution, residual, direction, along_dir, norm_now, step_size = carry
        solution = solution + step_size * direction
        residual = residual - step_size * along_dir
        applied = operate(residual)
        norm_next, product = both_sums(residual, applied)
        beta_ratio = norm_next / norm_now
        step_next = norm_next / (product - beta_ratio * norm_next / step_size)
        direction = residual + beta_ratio * direction
        along_dir = applied + beta_ratio * along_dir
        return (solution, residual, direction, along_dir, norm_next, step_next)

    carry = (solution, residual, residual, applied, norm_now, step_size)
    solution, residual, direction, along_dir, norm_now, step_size = lax.fori_loop(
        0, ITERS - 1, iterate, carry
    )
    solution = solution + step_size * direction
    sol_pad = padded_2(solution, (("strip", 2),), 1)
    sol_pad = jnp.pad(sol_pad, ((0, 0), (0, 0), (0, 0), (1, 1)))
    forward_field = solution[:, 0]
    adjoint_field = solution[:, 1]
    fwd_pad = sol_pad[:, 0]
    adj_pad = sol_pad[:, 1]
    term_up = jnp.where(
        top_keep[None],
        (forward_field - fwd_pad[:, :-2, 1:-1]) * (adjoint_field - adj_pad[:, :-2, 1:-1]),
        0.0,
    )
    term_down = (forward_field - fwd_pad[:, 2:, 1:-1]) * (adjoint_field - adj_pad[:, 2:, 1:-1])
    term_left = (forward_field - fwd_pad[:, 1:-1, :-2]) * (adjoint_field - adj_pad[:, 1:-1, :-2])
    term_right = (forward_field - fwd_pad[:, 1:-1, 2:]) * (adjoint_field - adj_pad[:, 1:-1, 2:])
    partial_value = (wavenum * wavenum)[:, None, None] * forward_field * adjoint_field + 0.5 * (
        term_up + term_down + term_left + term_right
    )
    local_sum = jnp.sum(weights[:, None, None] * partial_value, axis=0)
    summed = lax.psum(local_sum, "wave")
    share_width = cell_count // lax.axis_size("wave")
    share_out = lax.dynamic_slice_in_dim(
        summed, lax.axis_index("wave") * share_width, share_width, 1
    )
    return -share_out


LANES = 128
PAD = 8
ROWS = 64
FIRST = 1


def gathers_whole(shape):
    waves, _, rows, cells = shape
    strips = lax.axis_size("strip")
    return (
        lax.axis_size("wave") == 2
        and 2 * rows * strips == LANES
        and rows == PAD
        and strips >= waves + FIRST
        and cells % (2 * LANES) == 0
    )


def enter(peers):
    barrier = pltpu.get_barrier_semaphore()
    for peer in peers:
        pl.semaphore_signal(barrier, inc=1, device_id=peer, device_id_type=pl.DeviceIdType.MESH)
    pl.semaphore_wait(barrier, len(peers))


def strip_peers():
    strips = lax.axis_size("strip")
    strip = lax.axis_index("strip")
    return [{"strip": lax.rem(strip + hop, strips)} for hop in range(1, strips)]


def gather_kernel(prior, sigma, fields, section, sent, got, sigma_sent, sigma_got, own):
    strips = lax.axis_size("strip")
    strip = lax.axis_index("strip")
    waves = prior.shape[0]
    rows = sigma.shape[0]
    here = pl.ds(pl.multiple_of(strip * rows, PAD), rows)
    enter(strip_peers())

    def field_copy(place):
        return pltpu.make_async_remote_copy(
            src_ref=prior.at[place],
            dst_ref=fields.at[:, here, :],
            send_sem=sent.at[place],
            recv_sem=got.at[strip],
            device_id={"strip": place + FIRST},
            device_id_type=pl.DeviceIdType.MESH,
        )

    def sigma_copy(place):
        return pltpu.make_async_remote_copy(
            src_ref=sigma,
            dst_ref=section.at[here, :],
            send_sem=sigma_sent.at[place],
            recv_sem=sigma_got.at[strip],
            device_id={"strip": place + FIRST},
            device_id_type=pl.DeviceIdType.MESH,
        )

    def local_copies(place):
        return (
            pltpu.make_async_copy(prior.at[place], fields.at[:, here, :], own.at[0]),
            pltpu.make_async_copy(sigma, section.at[here, :], own.at[1]),
        )

    for place in range(waves):

        @pl.when(strip != place + FIRST)
        def _():
            sigma_copy(place).start()
            field_copy(place).start()

        @pl.when(strip == place + FIRST)
        def _():
            for copy in local_copies(place):
                copy.start()

    for place in range(waves):

        @pl.when(strip != place + FIRST)
        def _():
            sigma_copy(place).wait_send()
            field_copy(place).wait_send()

        @pl.when(strip == place + FIRST)
        def _():
            for copy in local_copies(place):
                copy.wait()
            for source in range(strips):
                if source != place + FIRST:
                    there = pl.ds(source * rows, rows)
                    pltpu.make_async_copy(
                        section.at[there, :], section.at[there, :], sigma_got.at[source]
                    ).wait()
                    pltpu.make_async_copy(
                        fields.at[:, there, :], fields.at[:, there, :], got.at[source]
                    ).wait()


def solve_kernel(
    nodes, pair, gains, scales, fields, section, out, x, d, r, q, s, diag, up, down, left
):
    half = r.shape[1]
    cells = 2 * half
    count = nodes.shape[0]
    step = 64
    square = scales[0]
    weight = scales[1]
    lane = lax.broadcasted_iota(jnp.int32, (PAD, LANES), 1)
    second = lane >= ROWS

    def swap(block):
        return pltpu.roll(block, ROWS, 1)

    def edges(ref):
        last = ref[pl.ds(half, PAD), :]
        ref[pl.ds(0, PAD), :] = jnp.where(second, swap(last), 0.0)
        first = ref[pl.ds(PAD, PAD), :]
        ref[pl.ds(half + PAD, PAD), :] = jnp.where(second, 0.0, swap(first))

    def turn(read, ref):
        for block in range(half // LANES):
            both = jnp.concatenate(
                [read(pl.ds(block * LANES, LANES)), read(pl.ds(half + block * LANES, LANES))], 0
            )
            ref[pl.ds(PAD + block * LANES, LANES), :] = both.T

    turn(lambda cols: section[:, cols], s)
    edges(s)
    for c in range(2):
        turn(lambda cols, c=c: fields[c, :, cols], x.at[c])
        edges(x.at[c])

    row_lane = lax.rem(lax.broadcasted_iota(jnp.int32, (step, LANES), 1), ROWS)
    top = row_lane == 0
    bottom = row_lane == ROWS - 1

    def rows(index, shift=0):
        return pl.ds(index * step + shift, step)

    @pl.loop(0, half // step)
    def _(i):
        here = s[rows(i, PAD), :]
        face_left = 0.5 * (here + s[rows(i, PAD - 1), :])
        face_right = 0.5 * (here + s[rows(i, PAD + 1), :])
        face_up = jnp.where(top, 0.0, 0.5 * (here + pltpu.roll(here, 1, 1)))
        below = jnp.where(bottom, 0.0, pltpu.roll(here, LANES - 1, 1))
        face_down = 0.5 * (here + below)
        diag[rows(i), :] = face_up + face_down + face_left + face_right + square * here
        up[rows(i), :] = face_up
        down[rows(i), :] = jnp.where(bottom, 0.0, face_down)
        left[rows(i), :] = face_left
        r[0, rows(i), :] = jnp.zeros_like(here)
        r[1, rows(i), :] = jnp.zeros_like(here)

    tail = s[pl.ds(half + PAD, PAD), :]
    left[pl.ds(half, PAD), :] = 0.5 * (tail + s[pl.ds(half + PAD - 1, PAD), :])

    line = lax.broadcasted_iota(jnp.int32, (1, LANES), 1)

    def put(c, electrode, value):
        node = nodes[electrode]
        row = lax.div(node, cells)
        col = lax.rem(node, cells)
        side = lax.div(col, half)
        at = pl.ds(lax.rem(col, half), 1)
        r[c, at, :] = r[c, at, :] + jnp.where(line == side * ROWS + row, value, 0.0)

    put(0, pair[0], 1.0)
    put(0, pair[1], -1.0)

    @pl.loop(0, count)
    def _(electrode):
        put(1, electrode, gains[electrode])

    def applied(ref, c, i):
        mid = ref[c, rows(i, PAD), :]
        result = diag[rows(i), :] * mid - up[rows(i), :] * pltpu.roll(mid, 1, 1)
        result = result - down[rows(i), :] * pltpu.roll(mid, LANES - 1, 1)
        result = result - left[rows(i), :] * ref[c, rows(i, PAD - 1), :]
        return mid, result - left[rows(i, 1), :] * ref[c, rows(i, PAD + 1), :]

    def fold(value):
        return jnp.sum(value.reshape(step // PAD, PAD, LANES), axis=0)

    def total(value):
        return jnp.sum(value, keepdims=True)

    none = (jnp.zeros((PAD, LANES), jnp.float32),) * 2

    def sweep(body, carry):
        return lax.fori_loop(0, half // step, body, carry)

    def start(i, sums):
        found = []
        for c in range(2):
            _, image = applied(x, c, i)
            value = r[c, rows(i), :] - image
            r[c, rows(i), :] = value
            d[c, rows(i, PAD), :] = value
            found.append(sums[c] + fold(value * value))
        return tuple(found)

    norm = tuple(total(value) for value in sweep(start, none))

    def images(i, sums):
        found = []
        for c in range(2):
            mid, image = applied(d, c, i)
            q[c, rows(i), :] = image
            found.append(sums[c] + fold(mid * image))
        return tuple(found)

    def step_sizes(norm):
        for c in range(2):
            edges(d.at[c])
        sums = sweep(images, none)
        return tuple(norm[c] / total(sums[c]) for c in range(2))

    def iterate(_, norm):
        size = step_sizes(norm)

        def reduce(i, sums):
            found = []
            for c in range(2):
                value = r[c, rows(i), :] - size[c] * q[c, rows(i), :]
                r[c, rows(i), :] = value
                found.append(sums[c] + fold(value * value))
            return tuple(found)

        after = tuple(total(value) for value in sweep(reduce, none))
        ratio = tuple(after[c] / norm[c] for c in range(2))

        @pl.loop(0, half // step)
        def _(i):
            for c in range(2):
                old = d[c, rows(i, PAD), :]
                x[c, rows(i, PAD), :] = x[c, rows(i, PAD), :] + size[c] * old
                d[c, rows(i, PAD), :] = r[c, rows(i), :] + ratio[c] * old

        return after

    norm = lax.fori_loop(0, ITERS - 1, iterate, norm)
    size = step_sizes(norm)

    @pl.loop(0, half // step)
    def _(i):
        for c in range(2):
            x[c, rows(i, PAD), :] = x[c, rows(i, PAD), :] + size[c] * d[c, rows(i, PAD), :]

    for c in range(2):
        edges(x.at[c])

    wide = lax.rem(lax.broadcasted_iota(jnp.int32, (LANES, LANES), 1), ROWS)

    @pl.loop(0, half // LANES)
    def _(b):
        base = pl.multiple_of(b * LANES, LANES)
        u = x[0, pl.ds(base + PAD, LANES), :]
        v = x[1, pl.ds(base + PAD, LANES), :]
        both = u * v
        term = (u - x[0, pl.ds(base + PAD - 1, LANES), :]) * (
            v - x[1, pl.ds(base + PAD - 1, LANES), :]
        )
        term = term + (u - x[0, pl.ds(base + PAD + 1, LANES), :]) * (
            v - x[1, pl.ds(base + PAD + 1, LANES), :]
        )
        rise = (u - pltpu.roll(u, 1, 1)) * (v - pltpu.roll(v, 1, 1))
        term = term + jnp.where(wide == 0, 0.0, rise)
        term = term + jnp.where(wide == ROWS - 1, both, pltpu.roll(rise, LANES - 1, 1))
        out[:, pl.ds(base, LANES)] = ((-weight) * (square * both + 0.5 * term)).T


def scatter_kernel(own, out, other, mine, parts, core_sent, core_got, sent, got):
    strips = lax.axis_size("strip")
    strip = lax.axis_index("strip")
    core = lax.axis_index("wave")
    waves = parts.shape[0]
    rows = out.shape[0]
    enter(strip_peers() + [{"wave": 1 - core}])
    solver = (strip >= FIRST) & (strip < FIRST + waves)

    swap = pltpu.make_async_remote_copy(
        src_ref=own.at[pl.ds(pl.multiple_of((1 - core) * ROWS, ROWS), ROWS), :],
        dst_ref=other,
        send_sem=core_sent,
        recv_sem=core_got,
        device_id={"wave": 1 - core},
        device_id_type=pl.DeviceIdType.MESH,
    )

    def part_copy(target):
        return pltpu.make_async_remote_copy(
            src_ref=mine.at[pl.ds(target * rows, rows), :],
            dst_ref=parts.at[strip - FIRST],
            send_sem=sent.at[target],
            recv_sem=got.at[strip - FIRST],
            device_id={"strip": target},
            device_id_type=pl.DeviceIdType.MESH,
        )

    @pl.when(solver)
    def _():
        swap.start()
        swap.wait_recv()
        mine[...] = own[pl.ds(pl.multiple_of(core * ROWS, ROWS), ROWS), :] + other[...]
        for target in range(strips):

            @pl.when(strip != target)
            def _():
                part_copy(target).start()

        parts[strip - FIRST] = mine[pl.ds(pl.multiple_of(strip * rows, rows), rows), :]

    for place in range(waves):

        @pl.when(strip != place + FIRST)
        def _():
            pltpu.make_async_copy(parts.at[place], parts.at[place], got.at[place]).wait()

    total = parts[0]
    for place in range(1, waves):
        total = total + parts[place]
    out[...] = total

    @pl.when(solver)
    def _():
        swap.wait_send()
        for target in range(strips):

            @pl.when(strip != target)
            def _():
                part_copy(target).wait_send()


def per_device_whole(prior_fields, conductivity, electrode_nodes, source_pair, innovation):
    waves, _, rows, cells = prior_fields.shape
    strips = lax.axis_size("strip")
    half = cells // 2
    vmem = pl.BlockSpec(memory_space=pltpu.VMEM)
    smem = pl.BlockSpec(memory_space=pltpu.SMEM)
    f32 = jnp.float32
    dma = pltpu.SemaphoreType.DMA

    fields, section = pl.pallas_call(
        gather_kernel,
        out_shape=(
            jax.ShapeDtypeStruct((2, ROWS, cells), f32),
            jax.ShapeDtypeStruct((ROWS, cells), f32),
        ),
        in_specs=[vmem, vmem],
        out_specs=(vmem, vmem),
        scratch_shapes=[
            dma((waves,)),
            dma((strips,)),
            dma((waves,)),
            dma((strips,)),
            dma((2,)),
        ],
        compiler_params=pltpu.CompilerParams(
            collective_id=0, has_side_effects=True, vmem_limit_bytes=32 * 2**20
        ),
        name="gather_sections",
    )(prior_fields, conductivity)

    wave_id = lax.axis_index("wave") * waves + lax.axis_index("strip") - FIRST
    wavenum, weights = wave_table(wave_id.astype(f32))
    scales = jnp.stack([wavenum * wavenum, weights])
    padded = half + 2 * PAD
    partial = pl.pallas_call(
        solve_kernel,
        out_shape=jax.ShapeDtypeStruct((LANES, half), f32),
        in_specs=[smem] * 4 + [vmem] * 2,
        out_specs=vmem,
        scratch_shapes=[
            pltpu.VMEM((2, padded, LANES), f32),
            pltpu.VMEM((2, padded, LANES), f32),
            pltpu.VMEM((2, half, LANES), f32),
            pltpu.VMEM((2, half, LANES), f32),
            pltpu.VMEM((padded, LANES), f32),
            pltpu.VMEM((half, LANES), f32),
            pltpu.VMEM((half, LANES), f32),
            pltpu.VMEM((half, LANES), f32),
            pltpu.VMEM((half + PAD, LANES), f32),
        ],
        compiler_params=pltpu.CompilerParams(vmem_limit_bytes=32 * 2**20),
        name="solve_wave",
    )(electrode_nodes, source_pair, innovation, scales, fields, section)

    return pl.pallas_call(
        scatter_kernel,
        out_shape=jax.ShapeDtypeStruct((rows, half), f32),
        in_specs=[vmem],
        out_specs=vmem,
        scratch_shapes=[
            pltpu.VMEM((ROWS, half), f32),
            pltpu.VMEM((ROWS, half), f32),
            pltpu.VMEM((waves, rows, half), f32),
            dma,
            dma,
            dma((strips,)),
            dma((waves,)),
        ],
        compiler_params=pltpu.CompilerParams(
            collective_id=1, has_side_effects=True, vmem_limit_bytes=32 * 2**20
        ),
        name="scatter_gradient",
    )(partial)


def solution(mesh):
    in_specs = (
        P("wave", None, ("lines", "strip"), None),
        P(("lines", "strip"), None),
        P("lines"),
        P("lines"),
        P("lines"),
    )
    out_specs = P(("lines", "strip"), "wave")

    def per_device(prior_fields, *rest):
        if gathers_whole(prior_fields.shape):
            return per_device_whole(prior_fields, *rest)
        return per_device_strips(prior_fields, *rest)

    return jax.shard_map(
        per_device, mesh=mesh, in_specs=in_specs, out_specs=out_specs, check_vma=False
    )
```

```python
import math

import jax
import jax.numpy as jnp
from jax import lax
from jax.experimental import pallas as pl
from jax.experimental.pallas import tpu as pltpu
from jax.sharding import PartitionSpec as P

WAVES = 12
ITERS = 12


k_lowest = 0.01
k_highest = 1.0


def padded_2(block, sides, width):
    for axis, dim in sides:
        count = lax.axis_size(axis)
        forward = [(i, i + 1) for i in range(count - 1)]
        backward = [(target, source) for source, target in forward]
        low = lax.ppermute(
            lax.slice_in_dim(block, block.shape[dim] - width, None, axis=dim), axis, forward
        )
        high = lax.ppermute(lax.slice_in_dim(block, 0, width, axis=dim), axis, backward)
        block = jnp.concatenate([low, block, high], axis=dim)
    return block


def wave_table(position):
    spacing = (math.log(k_highest) - math.log(k_lowest)) / (WAVES - 1)
    wavenum = jnp.exp(math.log(k_lowest) + spacing * position)
    ends = jnp.where((position == 0) | (position == WAVES - 1), 0.5, 1.0)
    weights = 2.0 / math.pi * spacing * wavenum * ends
    return (wavenum, weights)


def inner_sums(first, second):
    return jnp.sum(first * second, axis=(2, 3), keepdims=True)


def per_device_strips(prior_fields, conductivity, electrode_nodes, source_pair, innovation):
    wave_dev = prior_fields.shape[0]
    row_count = prior_fields.shape[2]
    cell_count = prior_fields.shape[3]
    row_ids = lax.axis_index("strip") * row_count + jnp.arange(row_count, dtype=jnp.int32)
    top_keep = (row_ids != 0)[:, None]
    sig_pad = padded_2(conductivity, (("strip", 0),), 1)
    sig_pad = jnp.pad(sig_pad, ((0, 0), (1, 1)))
    face_up = jnp.where(top_keep, 0.5 * (conductivity + sig_pad[:-2, 1:-1]), 0.0)
    face_down = 0.5 * (conductivity + sig_pad[2:, 1:-1])
    face_left = 0.5 * (conductivity + sig_pad[1:-1, :-2])
    face_right = 0.5 * (conductivity + sig_pad[1:-1, 2:])
    wave_ids = (lax.axis_index("wave") * wave_dev + jnp.arange(wave_dev, dtype=jnp.int32)).astype(
        jnp.float32
    )
    wavenum, weights = wave_table(wave_ids)
    face_sum = face_up + face_down + face_left + face_right
    diagonal = (face_sum[None] + (wavenum * wavenum)[:, None, None] * conductivity[None])[:, None]

    def operate(vector):
        padded = padded_2(vector, (("strip", 2),), 1)
        padded = jnp.pad(padded, ((0, 0), (0, 0), (0, 0), (1, 1)))
        result = diagonal * vector - face_up * padded[:, :, :-2, 1:-1]
        result = result - face_down * padded[:, :, 2:, 1:-1]
        result = result - face_left * padded[:, :, 1:-1, :-2]
        return result - face_right * padded[:, :, 1:-1, 2:]

    electrode_ids = jnp.arange(innovation.shape[0], dtype=jnp.int32)
    forward = (electrode_ids == source_pair[0]).astype(jnp.float32) - (
        electrode_ids == source_pair[1]
    ).astype(jnp.float32)
    values = jnp.stack([forward, innovation])
    node_rows = electrode_nodes // cell_count
    node_cols = electrode_nodes % cell_count
    rows_hot = (node_rows[:, None] == row_ids[None, :]).astype(jnp.float32)
    cols_hot = (node_cols[:, None] == jnp.arange(cell_count, dtype=jnp.int32)[None, :]).astype(
        jnp.float32
    )
    weighted = values[:, :, None] * rows_hot[None]
    source = jnp.einsum("sez,ex->szx", weighted, cols_hot, precision=lax.Precision.HIGHEST)[None]
    solution = prior_fields
    residual = source - operate(solution)

    def both_sums(vector, applied):
        return lax.psum((inner_sums(vector, vector), inner_sums(vector, applied)), "strip")

    applied = operate(residual)
    norm_now, product = both_sums(residual, applied)
    step_size = norm_now / product

    def iterate(sweep, carry):
        solution, residual, direction, along_dir, norm_now, step_size = carry
        solution = solution + step_size * direction
        residual = residual - step_size * along_dir
        applied = operate(residual)
        norm_next, product = both_sums(residual, applied)
        beta_ratio = norm_next / norm_now
        step_next = norm_next / (product - beta_ratio * norm_next / step_size)
        direction = residual + beta_ratio * direction
        along_dir = applied + beta_ratio * along_dir
        return (solution, residual, direction, along_dir, norm_next, step_next)

    carry = (solution, residual, residual, applied, norm_now, step_size)
    solution, residual, direction, along_dir, norm_now, step_size = lax.fori_loop(
        0, ITERS - 1, iterate, carry
    )
    solution = solution + step_size * direction
    sol_pad = padded_2(solution, (("strip", 2),), 1)
    sol_pad = jnp.pad(sol_pad, ((0, 0), (0, 0), (0, 0), (1, 1)))
    forward_field = solution[:, 0]
    adjoint_field = solution[:, 1]
    fwd_pad = sol_pad[:, 0]
    adj_pad = sol_pad[:, 1]
    term_up = jnp.where(
        top_keep[None],
        (forward_field - fwd_pad[:, :-2, 1:-1]) * (adjoint_field - adj_pad[:, :-2, 1:-1]),
        0.0,
    )
    term_down = (forward_field - fwd_pad[:, 2:, 1:-1]) * (adjoint_field - adj_pad[:, 2:, 1:-1])
    term_left = (forward_field - fwd_pad[:, 1:-1, :-2]) * (adjoint_field - adj_pad[:, 1:-1, :-2])
    term_right = (forward_field - fwd_pad[:, 1:-1, 2:]) * (adjoint_field - adj_pad[:, 1:-1, 2:])
    partial_value = (wavenum * wavenum)[:, None, None] * forward_field * adjoint_field + 0.5 * (
        term_up + term_down + term_left + term_right
    )
    local_sum = jnp.sum(weights[:, None, None] * partial_value, axis=0)
    summed = lax.psum(local_sum, "wave")
    share_width = cell_count // lax.axis_size("wave")
    share_out = lax.dynamic_slice_in_dim(
        summed, lax.axis_index("wave") * share_width, share_width, 1
    )
    return -share_out


LANES = 128
PAD = 8
ROWS = 64
FIRST = 1
STEP = 128


def gathers_whole(shape, electrodes):
    waves, _, rows, cells = shape
    strips = lax.axis_size("strip")
    return (
        lax.axis_size("wave") == 2
        and rows * strips == ROWS
        and rows == PAD
        and strips >= waves + FIRST
        and cells % (2 * STEP) == 0
        and cells // 2 >= 4 * STEP
        and electrodes <= LANES
    )


def whole_kernel(
    nodes, pair, gains, scales, prior, sigma, out,
    fields, section, x, past, q, w, s, diag, up, left, charge, steps, grad, other, mine, parts,
    sigma_sent, sigma_got, field_sent, field_got, own_sem, core_sent, core_got, sent, got,
):
    strips = lax.axis_size("strip")
    strip = lax.axis_index("strip")
    core = lax.axis_index("wave")
    waves = prior.shape[0]
    depth = sigma.shape[0]
    half = q.shape[0]
    cells = 2 * half
    blocks = half // STEP
    here = pl.ds(pl.multiple_of(strip * depth, PAD), depth)
    peer = {"wave": 1 - core}
    mesh_id = pl.DeviceIdType.MESH
    solver = (strip >= FIRST) & (strip < FIRST + waves)

    barrier = pltpu.get_barrier_semaphore()
    for hop in range(1, strips):
        pl.semaphore_signal(
            barrier, inc=1, device_id={"strip": lax.rem(strip + hop, strips)}, device_id_type=mesh_id
        )
    pl.semaphore_signal(barrier, inc=1, device_id=peer, device_id_type=mesh_id)
    pl.semaphore_wait(barrier, strips)

    def remote(src, dst, send_sem, recv_sem, device):
        return pltpu.make_async_remote_copy(
            src_ref=src,
            dst_ref=dst,
            send_sem=send_sem,
            recv_sem=recv_sem,
            device_id=device,
            device_id_type=mesh_id,
        )

    my_side = pl.ds(pl.multiple_of(core * half, LANES), half)

    def sigma_copy(place):
        return remote(
            sigma.at[:, my_side],
            section.at[core, here, :],
            sigma_sent.at[place],
            sigma_got.at[strip],
            {"strip": place + FIRST},
        )

    def field_copy(place, c):
        return remote(
            prior.at[place, c],
            fields.at[c, here, :],
            field_sent.at[c, place],
            field_got.at[c, strip],
            {"strip": place + FIRST},
        )

    def own_sigma():
        return pltpu.make_async_copy(
            sigma.at[:, my_side], section.at[core, here, :], own_sem.at[2]
        )

    def own_field(c):
        return pltpu.make_async_copy(
            prior.at[strip - FIRST, c], fields.at[c, here, :], own_sem.at[c]
        )

    def each_other(body):
        for place in range(waves):

            @pl.when(strip != place + FIRST)
            def _(place=place):
                body(place)

    def from_others(body):
        for source in range(strips):

            @pl.when(strip != source)
            def _(source=source):
                body(source)

    def await_block(ref, sem):
        pltpu.make_async_copy(ref, ref, sem).wait()

    each_other(lambda place: sigma_copy(place).start())
    each_other(lambda place: field_copy(place, 0).start())

    @pl.when(solver)
    def _():
        own_sigma().start()
        own_field(0).start()
        own_field(1).start()

    def send_second():
        each_other(lambda place: sigma_copy(place).wait_send())
        each_other(lambda place: field_copy(place, 0).wait_send())
        each_other(lambda place: field_copy(place, 1).start())

    square = scales[0]
    weight = scales[1]
    lane = lax.broadcasted_iota(jnp.int32, (PAD, LANES), 1)
    second = lane >= ROWS

    def swap(block):
        return pltpu.roll(block, ROWS, 1)

    def edges(ref):
        last = ref[pl.ds(half, PAD), :]
        ref[pl.ds(0, PAD), :] = jnp.where(second, swap(last), 0.0)
        first = ref[pl.ds(PAD, PAD), :]
        ref[pl.ds(half + PAD, PAD), :] = jnp.where(second, 0.0, swap(first))

    def rows(block, shift=0):
        return pl.ds(block * STEP + shift, STEP)

    def fold(value):
        return jnp.sum(value.reshape(STEP // PAD, PAD, LANES), axis=0)

    def total(value):
        return jnp.sum(value, keepdims=True)

    def charges():
        line = lax.broadcasted_iota(jnp.int32, (1, LANES), 1)
        charge[...] = jnp.zeros_like(charge)

        def mark(e, spots):
            node = nodes[e]
            col = lax.rem(node, cells)
            side = lax.div(col, half)
            hit = line == side * ROWS + lax.div(node, cells)
            sign = jnp.where(pair[0] == e, 1.0, 0.0) - jnp.where(pair[1] == e, 1.0, 0.0)
            charge[0, pl.ds(e, 1), :] = jnp.where(hit, sign, 0.0)
            charge[1, pl.ds(e, 1), :] = jnp.where(hit, gains[e], 0.0)
            return jnp.where(line == e, lax.rem(col, half), spots)

        return lax.fori_loop(0, nodes.shape[0], mark, jnp.full((1, LANES), -1, jnp.int32))

    def coefficients():
        row_lane = lax.rem(lax.broadcasted_iota(jnp.int32, (STEP, LANES), 1), ROWS)
        top = row_lane == 0
        bottom = row_lane == ROWS - 1
        for b in range(blocks):
            cols = pl.ds(b * STEP, STEP)
            s[rows(b, PAD), :] = jnp.concatenate([section[0, :, cols], section[1, :, cols]], 0).T
        edges(s)
        for b in range(blocks):
            mid = s[rows(b, PAD), :]
            face_left = 0.5 * (mid + s[rows(b, PAD - 1), :])
            face_right = 0.5 * (mid + s[rows(b, PAD + 1), :])
            up[rows(b), :] = jnp.where(top, 0.0, 0.5 * (mid + pltpu.roll(mid, 1, 1)))
            left[rows(b), :] = face_left
            floor = jnp.where(bottom, 0.5 * mid, 0.0)
            diag[rows(b), :] = face_left + face_right + floor + square * mid
        tail = s[pl.ds(half + PAD, PAD), :]
        left[pl.ds(half, PAD), :] = 0.5 * (tail + s[pl.ds(half + PAD - 1, PAD), :])

    def applied(ref, b):
        mid = ref[rows(b, PAD), :]
        flux = up[rows(b), :] * (mid - pltpu.roll(mid, 1, 1))
        result = diag[rows(b), :] * mid + (flux - pltpu.roll(flux, LANES - 1, 1))
        result = result - left[rows(b), :] * ref[rows(b, PAD - 1), :]
        return mid, result - left[rows(b, 1), :] * ref[rows(b, PAD + 1), :]

    def solve(c, spots):
        xc = x.at[c]
        for b in range(blocks):
            one = fields[c, :, pl.ds(b * STEP, STEP)]
            two = fields[c, :, pl.ds(half + b * STEP, STEP)]
            xc[rows(b, PAD), :] = jnp.concatenate([one, two], 0).T
        edges(xc)
        for b in range(blocks):
            cell = b * STEP + lax.broadcasted_iota(jnp.int32, (STEP, LANES), 0)
            source = jnp.dot(
                jnp.where(cell == spots, 1.0, 0.0),
                charge[c],
                precision=lax.Precision.HIGHEST,
                preferred_element_type=jnp.float32,
            )
            past[0, rows(b, PAD), :] = source - applied(xc, b)[1]
        edges(past.at[0])

        def image(ref, b, sums):
            mid, value = applied(ref, b)
            w[rows(b), :] = value
            return sums[0] + fold(mid * mid), sums[1] + fold(mid * value)

        none = (jnp.zeros((PAD, LANES), jnp.float32),) * 2
        sums = none
        for b in range(blocks):
            sums = image(past.at[0], b, sums)
        norm, product = total(sums[0]), total(sums[1])
        size = norm / product
        for b in range(blocks):
            q[rows(b), :] = jnp.zeros((STEP, LANES), jnp.float32)

        def wide(value):
            return jnp.broadcast_to(value, (1, LANES))

        steps[0, pl.ds(0, 1), :] = wide(size)

        def iterate(k, carry):
            norm, size, ratio = carry
            now = past.at[k]
            new = past.at[k + 1]

            def advance(b):
                along = w[rows(b), :] + ratio * q[rows(b), :]
                q[rows(b), :] = along
                new[rows(b, PAD), :] = now[rows(b, PAD), :] - size * along

            advance(blocks - 1)
            advance(0)
            edges(new)
            sums = none
            for b in range(blocks):
                if b + 1 < blocks - 1:
                    advance(b + 1)
                sums = image(new, b, sums)
            after, product = total(sums[0]), total(sums[1])
            ratio = after / norm
            size = after / (product - ratio * after / size)
            steps[0, pl.ds(k + 1, 1), :] = wide(size)
            steps[1, pl.ds(k + 1, 1), :] = wide(ratio)
            return after, size, ratio

        lax.fori_loop(0, ITERS - 1, iterate, (norm, size, jnp.zeros_like(norm)))
        gain = steps[0, pl.ds(ITERS - 1, 1), :]
        shares = [gain]
        for k in range(ITERS - 2, -1, -1):
            gain = steps[0, pl.ds(k, 1), :] + steps[1, pl.ds(k + 1, 1), :] * gain
            shares.insert(0, gain)
        for b in range(blocks):
            value = xc[rows(b, PAD), :]
            for k in range(ITERS):
                value = value + shares[k] * past[k, rows(b, PAD), :]
            xc[rows(b, PAD), :] = value
        edges(xc)

    core_swap = remote(section.at[core], section.at[core], core_sent.at[0], core_got.at[0], peer)
    grad_swap = remote(
        grad.at[pl.ds(pl.multiple_of((1 - core) * ROWS, ROWS), ROWS), :],
        other,
        core_sent.at[1],
        core_got.at[1],
        peer,
    )

    def part_copy(target):
        return remote(
            mine.at[pl.ds(target * depth, depth), :],
            parts.at[strip - FIRST],
            sent.at[target],
            got.at[strip - FIRST],
            {"strip": target},
        )

    @pl.when(jnp.logical_not(solver))
    def _():
        send_second()

    @pl.when(solver)
    def _():
        spots = charges()
        own_sigma().wait()
        from_others(
            lambda source: await_block(
                section.at[core, pl.ds(source * depth, depth), :], sigma_got.at[source]
            )
        )
        core_swap.start()
        core_swap.wait()
        coefficients()
        own_field(0).wait()
        from_others(
            lambda source: await_block(
                fields.at[0, pl.ds(source * depth, depth), :], field_got.at[0, source]
            )
        )
        send_second()
        solve(0, spots)
        own_field(1).wait()
        from_others(
            lambda source: await_block(
                fields.at[1, pl.ds(source * depth, depth), :], field_got.at[1, source]
            )
        )
        solve(1, spots)

        row_lane = lax.rem(lax.broadcasted_iota(jnp.int32, (STEP, LANES), 1), ROWS)
        for b in range(blocks):
            u = x[0, rows(b, PAD), :]
            v = x[1, rows(b, PAD), :]
            both = u * v
            term = (u - x[0, rows(b, PAD - 1), :]) * (v - x[1, rows(b, PAD - 1), :])
            term = term + (u - x[0, rows(b, PAD + 1), :]) * (v - x[1, rows(b, PAD + 1), :])
            rise = (u - pltpu.roll(u, 1, 1)) * (v - pltpu.roll(v, 1, 1))
            term = term + jnp.where(row_lane == 0, 0.0, rise)
            fall = pltpu.roll(rise, LANES - 1, 1)
            term = term + jnp.where(row_lane == ROWS - 1, both, fall)
            grad[:, pl.ds(b * STEP, STEP)] = ((-weight) * (square * both + 0.5 * term)).T

        grad_swap.start()
        grad_swap.wait_recv()
        mine[...] = grad[pl.ds(pl.multiple_of(core * ROWS, ROWS), ROWS), :] + other[...]
        for target in range(strips):

            @pl.when(strip != target)
            def _():
                part_copy(target).start()

        parts[strip - FIRST] = mine[here, :]

    for place in range(waves):

        @pl.when(strip != place + FIRST)
        def _():
            await_block(parts.at[place], got.at[place])

    result = parts[0]
    for place in range(1, waves):
        result = result + parts[place]
    out[...] = result

    each_other(lambda place: field_copy(place, 1).wait_send())

    @pl.when(solver)
    def _():
        grad_swap.wait_send()
        for target in range(strips):

            @pl.when(strip != target)
            def _():
                part_copy(target).wait_send()


def per_device_whole(prior_fields, conductivity, electrode_nodes, source_pair, innovation):
    waves, _, rows, cells = prior_fields.shape
    strips = lax.axis_size("strip")
    half = cells // 2
    padded = half + 2 * PAD
    vmem = pl.BlockSpec(memory_space=pltpu.VMEM)
    smem = pl.BlockSpec(memory_space=pltpu.SMEM)
    anywhere = pl.BlockSpec(memory_space=pl.ANY)
    f32 = jnp.float32
    dma = pltpu.SemaphoreType.DMA

    wave_id = lax.axis_index("wave") * waves + lax.axis_index("strip") - FIRST
    wavenum, weights = wave_table(wave_id.astype(f32))
    scales = jnp.stack([wavenum * wavenum, weights])
    return pl.pallas_call(
        whole_kernel,
        out_shape=jax.ShapeDtypeStruct((rows, half), f32),
        in_specs=[smem] * 4 + [anywhere] * 2,
        out_specs=vmem,
        scratch_shapes=[
            pltpu.VMEM((2, ROWS, cells), f32),
            pltpu.VMEM((2, ROWS, half), f32),
            pltpu.VMEM((2, padded, LANES), f32),
            pltpu.VMEM((ITERS, padded, LANES), f32),
            pltpu.VMEM((half, LANES), f32),
            pltpu.VMEM((half, LANES), f32),
            pltpu.VMEM((padded, LANES), f32),
            pltpu.VMEM((half, LANES), f32),
            pltpu.VMEM((half, LANES), f32),
            pltpu.VMEM((half + PAD, LANES), f32),
            pltpu.VMEM((2, LANES, LANES), f32),
            pltpu.VMEM((2, 2 * PAD, LANES), f32),
            pltpu.VMEM((LANES, half), f32),
            pltpu.VMEM((ROWS, half), f32),
            pltpu.VMEM((ROWS, half), f32),
            pltpu.VMEM((waves, rows, half), f32),
            dma((waves,)),
            dma((strips,)),
            dma((2, waves)),
            dma((2, strips)),
            dma((3,)),
            dma((2,)),
            dma((2,)),
            dma((strips,)),
            dma((waves,)),
        ],
        compiler_params=pltpu.CompilerParams(
            collective_id=0, has_side_effects=True, vmem_limit_bytes=40 * 2**20
        ),
        name="solve_wave",
    )(electrode_nodes, source_pair, innovation, scales, prior_fields, conductivity)


def solution(mesh):
    in_specs = (
        P("wave", None, ("lines", "strip"), None),
        P(("lines", "strip"), None),
        P("lines"),
        P("lines"),
        P("lines"),
    )
    out_specs = P(("lines", "strip"), "wave")

    def per_device(prior_fields, *rest):
        if gathers_whole(prior_fields.shape, rest[-1].shape[0]):
            return per_device_whole(prior_fields, *rest)
        return per_device_strips(prior_fields, *rest)

    return jax.shard_map(
        per_device, mesh=mesh, in_specs=in_specs, out_specs=out_specs, check_vma=False
    )
```

```python
import math

import jax
import jax.numpy as jnp
from jax import lax
from jax.experimental import pallas as pl
from jax.experimental.pallas import tpu as pltpu
from jax.sharding import PartitionSpec as P

WAVES = 12
ITERS = 12


k_lowest = 0.01
k_highest = 1.0


def padded_2(block, sides, width):
    for axis, dim in sides:
        count = lax.axis_size(axis)
        forward = [(i, i + 1) for i in range(count - 1)]
        backward = [(target, source) for source, target in forward]
        low = lax.ppermute(
            lax.slice_in_dim(block, block.shape[dim] - width, None, axis=dim), axis, forward
        )
        high = lax.ppermute(lax.slice_in_dim(block, 0, width, axis=dim), axis, backward)
        block = jnp.concatenate([low, block, high], axis=dim)
    return block


def wave_table(position):
    spacing = (math.log(k_highest) - math.log(k_lowest)) / (WAVES - 1)
    wavenum = jnp.exp(math.log(k_lowest) + spacing * position)
    ends = jnp.where((position == 0) | (position == WAVES - 1), 0.5, 1.0)
    weights = 2.0 / math.pi * spacing * wavenum * ends
    return (wavenum, weights)


def inner_sums(first, second):
    return jnp.sum(first * second, axis=(2, 3), keepdims=True)


def per_device_strips(prior_fields, conductivity, electrode_nodes, source_pair, innovation):
    wave_dev = prior_fields.shape[0]
    row_count = prior_fields.shape[2]
    cell_count = prior_fields.shape[3]
    row_ids = lax.axis_index("strip") * row_count + jnp.arange(row_count, dtype=jnp.int32)
    top_keep = (row_ids != 0)[:, None]
    sig_pad = padded_2(conductivity, (("strip", 0),), 1)
    sig_pad = jnp.pad(sig_pad, ((0, 0), (1, 1)))
    face_up = jnp.where(top_keep, 0.5 * (conductivity + sig_pad[:-2, 1:-1]), 0.0)
    face_down = 0.5 * (conductivity + sig_pad[2:, 1:-1])
    face_left = 0.5 * (conductivity + sig_pad[1:-1, :-2])
    face_right = 0.5 * (conductivity + sig_pad[1:-1, 2:])
    wave_ids = (lax.axis_index("wave") * wave_dev + jnp.arange(wave_dev, dtype=jnp.int32)).astype(
        jnp.float32
    )
    wavenum, weights = wave_table(wave_ids)
    face_sum = face_up + face_down + face_left + face_right
    diagonal = (face_sum[None] + (wavenum * wavenum)[:, None, None] * conductivity[None])[:, None]

    def operate(vector):
        padded = padded_2(vector, (("strip", 2),), 1)
        padded = jnp.pad(padded, ((0, 0), (0, 0), (0, 0), (1, 1)))
        result = diagonal * vector - face_up * padded[:, :, :-2, 1:-1]
        result = result - face_down * padded[:, :, 2:, 1:-1]
        result = result - face_left * padded[:, :, 1:-1, :-2]
        return result - face_right * padded[:, :, 1:-1, 2:]

    electrode_ids = jnp.arange(innovation.shape[0], dtype=jnp.int32)
    forward = (electrode_ids == source_pair[0]).astype(jnp.float32) - (
        electrode_ids == source_pair[1]
    ).astype(jnp.float32)
    values = jnp.stack([forward, innovation])
    node_rows = electrode_nodes // cell_count
    node_cols = electrode_nodes % cell_count
    rows_hot = (node_rows[:, None] == row_ids[None, :]).astype(jnp.float32)
    cols_hot = (node_cols[:, None] == jnp.arange(cell_count, dtype=jnp.int32)[None, :]).astype(
        jnp.float32
    )
    weighted = values[:, :, None] * rows_hot[None]
    source = jnp.einsum("sez,ex->szx", weighted, cols_hot, precision=lax.Precision.HIGHEST)[None]
    solution = prior_fields
    residual = source - operate(solution)

    def both_sums(vector, applied):
        return lax.psum((inner_sums(vector, vector), inner_sums(vector, applied)), "strip")

    applied = operate(residual)
    norm_now, product = both_sums(residual, applied)
    step_size = norm_now / product

    def iterate(sweep, carry):
        solution, residual, direction, along_dir, norm_now, step_size = carry
        solution = solution + step_size * direction
        residual = residual - step_size * along_dir
        applied = operate(residual)
        norm_next, product = both_sums(residual, applied)
        beta_ratio = norm_next / norm_now
        step_next = norm_next / (product - beta_ratio * norm_next / step_size)
        direction = residual + beta_ratio * direction
        along_dir = applied + beta_ratio * along_dir
        return (solution, residual, direction, along_dir, norm_next, step_next)

    carry = (solution, residual, residual, applied, norm_now, step_size)
    solution, residual, direction, along_dir, norm_now, step_size = lax.fori_loop(
        0, ITERS - 1, iterate, carry
    )
    solution = solution + step_size * direction
    sol_pad = padded_2(solution, (("strip", 2),), 1)
    sol_pad = jnp.pad(sol_pad, ((0, 0), (0, 0), (0, 0), (1, 1)))
    forward_field = solution[:, 0]
    adjoint_field = solution[:, 1]
    fwd_pad = sol_pad[:, 0]
    adj_pad = sol_pad[:, 1]
    term_up = jnp.where(
        top_keep[None],
        (forward_field - fwd_pad[:, :-2, 1:-1]) * (adjoint_field - adj_pad[:, :-2, 1:-1]),
        0.0,
    )
    term_down = (forward_field - fwd_pad[:, 2:, 1:-1]) * (adjoint_field - adj_pad[:, 2:, 1:-1])
    term_left = (forward_field - fwd_pad[:, 1:-1, :-2]) * (adjoint_field - adj_pad[:, 1:-1, :-2])
    term_right = (forward_field - fwd_pad[:, 1:-1, 2:]) * (adjoint_field - adj_pad[:, 1:-1, 2:])
    partial_value = (wavenum * wavenum)[:, None, None] * forward_field * adjoint_field + 0.5 * (
        term_up + term_down + term_left + term_right
    )
    local_sum = jnp.sum(weights[:, None, None] * partial_value, axis=0)
    summed = lax.psum(local_sum, "wave")
    share_width = cell_count // lax.axis_size("wave")
    share_out = lax.dynamic_slice_in_dim(
        summed, lax.axis_index("wave") * share_width, share_width, 1
    )
    return -share_out


LANES = 128
PAD = 8
ROWS = 64
FIRST = 1
STEP = 256


def gathers_whole(shape, electrodes):
    waves, _, rows, cells = shape
    strips = lax.axis_size("strip")
    return (
        lax.axis_size("wave") == 2
        and rows * strips == ROWS
        and rows == PAD
        and strips >= waves + FIRST
        and cells == 2 * PAD * LANES
        and electrodes <= LANES
    )


def whole_kernel(
    nodes, pair, gains, scales, prior, sigma, out,
    fields, section, x, past, r, q, w, s, diag, up, left, charge, source, steps, grad, other, mine, parts,
    sigma_sent, sigma_got, field_sent, field_got, own_sem, core_sent, core_got, sent, got,
):
    strips = lax.axis_size("strip")
    strip = lax.axis_index("strip")
    core = lax.axis_index("wave")
    waves = prior.shape[0]
    depth = sigma.shape[0]
    half = q.shape[0]
    cells = 2 * half
    blocks = half // STEP
    here = pl.ds(pl.multiple_of(strip * depth, PAD), depth)
    peer = {"wave": 1 - core}
    mesh_id = pl.DeviceIdType.MESH
    solver = (strip >= FIRST) & (strip < FIRST + waves)

    barrier = pltpu.get_barrier_semaphore()
    for hop in range(1, strips):
        pl.semaphore_signal(
            barrier, inc=1, device_id={"strip": lax.rem(strip + hop, strips)}, device_id_type=mesh_id
        )
    pl.semaphore_signal(barrier, inc=1, device_id=peer, device_id_type=mesh_id)
    pl.semaphore_wait(barrier, strips)

    def remote(src, dst, send_sem, recv_sem, device):
        return pltpu.make_async_remote_copy(
            src_ref=src,
            dst_ref=dst,
            send_sem=send_sem,
            recv_sem=recv_sem,
            device_id=device,
            device_id_type=mesh_id,
        )

    my_side = pl.ds(pl.multiple_of(core * half, LANES), half)

    def sigma_copy(place):
        return remote(
            sigma.at[:, my_side],
            section.at[core, here, :],
            sigma_sent.at[place],
            sigma_got.at[strip],
            {"strip": place + FIRST},
        )

    def field_copy(place, c):
        return remote(
            prior.at[place, c],
            fields.at[c, here, :],
            field_sent.at[c, place],
            field_got.at[c, strip],
            {"strip": place + FIRST},
        )

    def own_sigma():
        return pltpu.make_async_copy(
            sigma.at[:, my_side], section.at[core, here, :], own_sem.at[2]
        )

    def own_field(c):
        return pltpu.make_async_copy(
            prior.at[strip - FIRST, c], fields.at[c, here, :], own_sem.at[c]
        )

    def each_other(body):
        for place in range(waves):

            @pl.when(strip != place + FIRST)
            def _(place=place):
                body(place)

    def from_others(body):
        for source in range(strips):

            @pl.when(strip != source)
            def _(source=source):
                body(source)

    def await_block(ref, sem):
        pltpu.make_async_copy(ref, ref, sem).wait()

    each_other(lambda place: sigma_copy(place).start())
    each_other(lambda place: field_copy(place, 0).start())
    @pl.when(solver)
    def _():
        own_sigma().start()
        own_field(0).start()
        own_field(1).start()

    def send_second():
        each_other(lambda place: sigma_copy(place).wait_send())
        each_other(lambda place: field_copy(place, 0).wait_send())
        each_other(lambda place: field_copy(place, 1).start())

    square = scales[0]
    weight = scales[1]
    lane = lax.broadcasted_iota(jnp.int32, (PAD, LANES), 1)
    second = lane >= ROWS
    band = lax.broadcasted_iota(jnp.int32, (PAD, LANES), 0)

    def swap(block):
        return pltpu.roll(block, ROWS, 1)

    def edges(ref):
        last = pltpu.roll(ref[pl.ds(half, PAD), :], 1, 0)
        ref[pl.ds(0, PAD), :] = jnp.where(
            band == 0, jnp.where(second, swap(last), 0.0), last
        )
        first = pltpu.roll(ref[pl.ds(PAD, PAD), :], PAD - 1, 0)
        ref[pl.ds(half + PAD, PAD), :] = jnp.where(
            band == PAD - 1, jnp.where(second, 0.0, swap(first)), first
        )

    def window(ref, block, shifts):
        tall = ref[pl.ds(block * STEP, STEP + (shifts - 1) * PAD), :]
        return [tall[shift * PAD : shift * PAD + STEP] for shift in range(shifts)]

    def turned(ref, read):
        for b in range(PAD):
            cols = pl.ds(b * LANES, LANES)
            more = pl.ds(half + b * LANES, LANES)
            both = jnp.concatenate([read(0, cols), read(1, more)], 0)
            ref[pl.ds(PAD + b, LANES, stride=PAD), :] = both.T

    def rows(block, shift=0):
        return pl.ds(block * STEP + shift, STEP)

    def fold(value):
        return jnp.sum(value.reshape(STEP // PAD, PAD, LANES), axis=0)

    def total(value):
        return jnp.sum(value, keepdims=True)

    def charges():
        line = lax.broadcasted_iota(jnp.int32, (1, LANES), 1)
        charge[...] = jnp.zeros_like(charge)

        def mark(e, spots):
            node = nodes[e]
            col = lax.rem(node, cells)
            side = lax.div(col, half)
            hit = line == side * ROWS + lax.div(node, cells)
            sign = jnp.where(pair[0] == e, 1.0, 0.0) - jnp.where(pair[1] == e, 1.0, 0.0)
            charge[0, pl.ds(e, 1), :] = jnp.where(hit, sign, 0.0)
            charge[1, pl.ds(e, 1), :] = jnp.where(hit, gains[e], 0.0)
            cell = lax.rem(col, half)
            spot = lax.rem(cell, LANES) * PAD + lax.div(cell, LANES)
            return jnp.where(line == e, spot, spots)

        return lax.fori_loop(0, nodes.shape[0], mark, jnp.full((1, LANES), -1, jnp.int32))

    def coefficients():
        row_lane = lax.rem(lax.broadcasted_iota(jnp.int32, (STEP, LANES), 1), ROWS)
        top = row_lane == 0
        bottom = row_lane == ROWS - 1
        turned(s, lambda side, cols: section[side, :, pl.ds(cols.start - side * half, LANES)])
        edges(s)
        for b in range(blocks):
            before, mid, after = window(s, b, 3)
            face_left = 0.5 * (mid + before)
            face_right = 0.5 * (mid + after)
            up[rows(b), :] = jnp.where(top, 0.0, 0.5 * (mid + pltpu.roll(mid, 1, 1)))
            left[rows(b), :] = face_left
            floor = jnp.where(bottom, 0.5 * mid, 0.0)
            diag[rows(b), :] = face_left + face_right + floor + square * mid
        tail = s[pl.ds(half + PAD, PAD), :]
        left[pl.ds(half, PAD), :] = 0.5 * (tail + s[pl.ds(half, PAD), :])

    def applied(ref, b):
        before, mid, after = window(ref, b, 3)
        face_left, face_right = window(left, b, 2)
        flux = up[rows(b), :] * (mid - pltpu.roll(mid, 1, 1))
        result = diag[rows(b), :] * mid + (flux - pltpu.roll(flux, LANES - 1, 1))
        return mid, result - face_left * before - face_right * after

    def sources(spots):
        for c in range(2):
            for b in range(blocks):
                cell = b * STEP + lax.broadcasted_iota(jnp.int32, (STEP, LANES), 0)
                source[c, rows(b), :] = jnp.dot(
                    jnp.where(cell == spots, 1.0, 0.0),
                    charge[c],
                    precision=lax.Precision.HIGHEST,
                    preferred_element_type=jnp.float32,
                )

    def solve(c):
        xc = x.at[c]
        turned(xc, lambda _, cols: fields[c, :, cols])
        edges(xc)
        for b in range(blocks):
            value = source[c, rows(b), :] - applied(xc, b)[1]
            r[rows(b, PAD), :] = value
            past[0, rows(b), :] = value
        edges(r)

        def image(b, sums):
            mid, value = applied(r, b)
            w[rows(b), :] = value
            return sums[0] + fold(mid * mid), sums[1] + fold(mid * value)

        none = (jnp.zeros((PAD, LANES), jnp.float32),) * 2
        sums = none
        for b in range(blocks):
            sums = image(b, sums)
        norm, product = total(sums[0]), total(sums[1])
        size = norm / product
        for b in range(blocks):
            q[rows(b), :] = jnp.zeros((STEP, LANES), jnp.float32)

        def wide(value):
            return jnp.broadcast_to(value, (1, LANES))

        steps[0, pl.ds(0, 1), :] = wide(size)

        def iterate(k, carry):
            norm, size, ratio = carry
            per_norm, per_size = 1.0 / norm, 1.0 / size

            def advance(b):
                along = w[rows(b), :] + ratio * q[rows(b), :]
                q[rows(b), :] = along
                value = r[rows(b, PAD), :] - size * along
                r[rows(b, PAD), :] = value
                past[k + 1, rows(b), :] = value

            advance(blocks - 1)
            advance(0)
            edges(r)
            sums = none
            for b in range(blocks):
                if b + 1 < blocks - 1:
                    advance(b + 1)
                sums = image(b, sums)
            after, product = total(sums[0]), total(sums[1])
            ratio = after * per_norm
            size = after / (product - ratio * after * per_size)
            steps[0, pl.ds(k + 1, 1), :] = wide(size)
            steps[1, pl.ds(k + 1, 1), :] = wide(ratio)
            return after, size, ratio

        lax.fori_loop(0, ITERS - 1, iterate, (norm, size, jnp.zeros_like(norm)))
        gain = steps[0, pl.ds(ITERS - 1, 1), :]
        shares = [gain]
        for k in range(ITERS - 2, -1, -1):
            gain = steps[0, pl.ds(k, 1), :] + steps[1, pl.ds(k + 1, 1), :] * gain
            shares.insert(0, gain)
        for b in range(blocks):
            value = xc[rows(b, PAD), :]
            for k in range(ITERS):
                value = value + shares[k] * past[k, rows(b), :]
            xc[rows(b, PAD), :] = value
        edges(xc)

    core_swap = remote(section.at[core], section.at[core], core_sent.at[0], core_got.at[0], peer)
    grad_swap = remote(
        grad.at[pl.ds(pl.multiple_of((1 - core) * ROWS, ROWS), ROWS), :],
        other,
        core_sent.at[1],
        core_got.at[1],
        peer,
    )

    def part_copy(target):
        return remote(
            mine.at[pl.ds(target * depth, depth), :],
            parts.at[strip - FIRST],
            sent.at[target],
            got.at[strip - FIRST],
            {"strip": target},
        )

    @pl.when(jnp.logical_not(solver))
    def _():
        send_second()

    @pl.when(solver)
    def _():
        sources(charges())
        own_sigma().wait()
        from_others(
            lambda source: await_block(
                section.at[core, pl.ds(source * depth, depth), :], sigma_got.at[source]
            )
        )
        core_swap.start()
        core_swap.wait()
        send_second()
        coefficients()
        own_field(0).wait()
        from_others(
            lambda source: await_block(
                fields.at[0, pl.ds(source * depth, depth), :], field_got.at[0, source]
            )
        )
        solve(0)
        own_field(1).wait()
        from_others(
            lambda source: await_block(
                fields.at[1, pl.ds(source * depth, depth), :], field_got.at[1, source]
            )
        )
        solve(1)

        row_lane = lax.rem(lax.broadcasted_iota(jnp.int32, (STEP, LANES), 1), ROWS)
        for b in range(blocks):
            u_before, u, u_after = window(x.at[0], b, 3)
            v_before, v, v_after = window(x.at[1], b, 3)
            both = u * v
            term = (u - u_before) * (v - v_before)
            term = term + (u - u_after) * (v - v_after)
            rise = (u - pltpu.roll(u, 1, 1)) * (v - pltpu.roll(v, 1, 1))
            term = term + jnp.where(row_lane == 0, 0.0, rise)
            fall = pltpu.roll(rise, LANES - 1, 1)
            term = term + jnp.where(row_lane == ROWS - 1, both, fall)
            w[rows(b), :] = (-weight) * (square * both + 0.5 * term)
        for b in range(PAD):
            grad[:, pl.ds(b * LANES, LANES)] = w[pl.ds(b, LANES, stride=PAD), :].T

        grad_swap.start()
        grad_swap.wait_recv()
        mine[...] = grad[pl.ds(pl.multiple_of(core * ROWS, ROWS), ROWS), :] + other[...]
        for target in range(strips):

            @pl.when(strip != target)
            def _():
                part_copy(target).start()

        parts[strip - FIRST] = mine[here, :]

    for place in range(waves):

        @pl.when(strip != place + FIRST)
        def _():
            await_block(parts.at[place], got.at[place])

    result = parts[0]
    for place in range(1, waves):
        result = result + parts[place]
    out[...] = result

    each_other(lambda place: field_copy(place, 1).wait_send())

    @pl.when(solver)
    def _():
        grad_swap.wait_send()
        for target in range(strips):

            @pl.when(strip != target)
            def _():
                part_copy(target).wait_send()


def per_device_whole(prior_fields, conductivity, electrode_nodes, source_pair, innovation):
    waves, _, rows, cells = prior_fields.shape
    strips = lax.axis_size("strip")
    half = cells // 2
    padded = half + 2 * PAD
    vmem = pl.BlockSpec(memory_space=pltpu.VMEM)
    smem = pl.BlockSpec(memory_space=pltpu.SMEM)
    anywhere = pl.BlockSpec(memory_space=pltpu.HBM)
    f32 = jnp.float32
    dma = pltpu.SemaphoreType.DMA

    wave_id = lax.axis_index("wave") * waves + lax.axis_index("strip") - FIRST
    wavenum, weights = wave_table(wave_id.astype(f32))
    scales = jnp.stack([wavenum * wavenum, weights])
    return pl.pallas_call(
        whole_kernel,
        out_shape=jax.ShapeDtypeStruct((rows, half), f32),
        in_specs=[smem] * 4 + [anywhere] * 2,
        out_specs=vmem,
        scratch_shapes=[
            pltpu.VMEM((2, ROWS, cells), f32),
            pltpu.VMEM((2, ROWS, half), f32),
            pltpu.VMEM((2, padded, LANES), f32),
            pltpu.VMEM((ITERS, half, LANES), f32),
            pltpu.VMEM((padded, LANES), f32),
            pltpu.VMEM((half, LANES), f32),
            pltpu.VMEM((half, LANES), f32),
            pltpu.VMEM((padded, LANES), f32),
            pltpu.VMEM((half, LANES), f32),
            pltpu.VMEM((half, LANES), f32),
            pltpu.VMEM((half + PAD, LANES), f32),
            pltpu.VMEM((2, LANES, LANES), f32),
            pltpu.VMEM((2, half, LANES), f32),
            pltpu.VMEM((2, 2 * PAD, LANES), f32),
            pltpu.VMEM((LANES, half), f32),
            pltpu.VMEM((ROWS, half), f32),
            pltpu.VMEM((ROWS, half), f32),
            pltpu.VMEM((waves, rows, half), f32),
            dma((waves,)),
            dma((strips,)),
            dma((2, waves)),
            dma((2, strips)),
            dma((3,)),
            dma((2,)),
            dma((2,)),
            dma((strips,)),
            dma((waves,)),
        ],
        compiler_params=pltpu.CompilerParams(
            collective_id=0, has_side_effects=True, vmem_limit_bytes=63 * 2**20
        ),
        name="solve_wave",
    )(electrode_nodes, source_pair, innovation, scales, prior_fields, conductivity)


def solution(mesh):
    in_specs = (
        P("wave", None, ("lines", "strip"), None),
        P(("lines", "strip"), None),
        P("lines"),
        P("lines"),
        P("lines"),
    )
    out_specs = P(("lines", "strip"), "wave")

    def per_device(prior_fields, *rest):
        if gathers_whole(prior_fields.shape, rest[-1].shape[0]):
            return per_device_whole(prior_fields, *rest)
        return per_device_strips(prior_fields, *rest)

    return jax.shard_map(
        per_device, mesh=mesh, in_specs=in_specs, out_specs=out_specs, check_vma=False
    )
```

```python
import math

import jax
import jax.numpy as jnp
from jax import lax
from jax.experimental import pallas as pl
from jax.experimental.pallas import tpu as pltpu
from jax.sharding import PartitionSpec as P

WAVES = 12
ITERS = 12


k_lowest = 0.01
k_highest = 1.0


def padded_2(block, sides, width):
    for axis, dim in sides:
        count = lax.axis_size(axis)
        forward = [(i, i + 1) for i in range(count - 1)]
        backward = [(target, source) for source, target in forward]
        low = lax.ppermute(
            lax.slice_in_dim(block, block.shape[dim] - width, None, axis=dim), axis, forward
        )
        high = lax.ppermute(lax.slice_in_dim(block, 0, width, axis=dim), axis, backward)
        block = jnp.concatenate([low, block, high], axis=dim)
    return block


def wave_table(position):
    spacing = (math.log(k_highest) - math.log(k_lowest)) / (WAVES - 1)
    wavenum = jnp.exp(math.log(k_lowest) + spacing * position)
    ends = jnp.where((position == 0) | (position == WAVES - 1), 0.5, 1.0)
    weights = 2.0 / math.pi * spacing * wavenum * ends
    return (wavenum, weights)


def inner_sums(first, second):
    return jnp.sum(first * second, axis=(2, 3), keepdims=True)


def per_device_strips(prior_fields, conductivity, electrode_nodes, source_pair, innovation):
    wave_dev = prior_fields.shape[0]
    row_count = prior_fields.shape[2]
    cell_count = prior_fields.shape[3]
    row_ids = lax.axis_index("strip") * row_count + jnp.arange(row_count, dtype=jnp.int32)
    top_keep = (row_ids != 0)[:, None]
    sig_pad = padded_2(conductivity, (("strip", 0),), 1)
    sig_pad = jnp.pad(sig_pad, ((0, 0), (1, 1)))
    face_up = jnp.where(top_keep, 0.5 * (conductivity + sig_pad[:-2, 1:-1]), 0.0)
    face_down = 0.5 * (conductivity + sig_pad[2:, 1:-1])
    face_left = 0.5 * (conductivity + sig_pad[1:-1, :-2])
    face_right = 0.5 * (conductivity + sig_pad[1:-1, 2:])
    wave_ids = (lax.axis_index("wave") * wave_dev + jnp.arange(wave_dev, dtype=jnp.int32)).astype(
        jnp.float32
    )
    wavenum, weights = wave_table(wave_ids)
    face_sum = face_up + face_down + face_left + face_right
    diagonal = (face_sum[None] + (wavenum * wavenum)[:, None, None] * conductivity[None])[:, None]

    def operate(vector):
        padded = padded_2(vector, (("strip", 2),), 1)
        padded = jnp.pad(padded, ((0, 0), (0, 0), (0, 0), (1, 1)))
        result = diagonal * vector - face_up * padded[:, :, :-2, 1:-1]
        result = result - face_down * padded[:, :, 2:, 1:-1]
        result = result - face_left * padded[:, :, 1:-1, :-2]
        return result - face_right * padded[:, :, 1:-1, 2:]

    electrode_ids = jnp.arange(innovation.shape[0], dtype=jnp.int32)
    forward = (electrode_ids == source_pair[0]).astype(jnp.float32) - (
        electrode_ids == source_pair[1]
    ).astype(jnp.float32)
    values = jnp.stack([forward, innovation])
    node_rows = electrode_nodes // cell_count
    node_cols = electrode_nodes % cell_count
    rows_hot = (node_rows[:, None] == row_ids[None, :]).astype(jnp.float32)
    cols_hot = (node_cols[:, None] == jnp.arange(cell_count, dtype=jnp.int32)[None, :]).astype(
        jnp.float32
    )
    weighted = values[:, :, None] * rows_hot[None]
    source = jnp.einsum("sez,ex->szx", weighted, cols_hot, precision=lax.Precision.HIGHEST)[None]
    solution = prior_fields
    residual = source - operate(solution)

    def both_sums(vector, applied):
        return lax.psum((inner_sums(vector, vector), inner_sums(vector, applied)), "strip")

    applied = operate(residual)
    norm_now, product = both_sums(residual, applied)
    step_size = norm_now / product

    def iterate(sweep, carry):
        solution, residual, direction, along_dir, norm_now, step_size = carry
        solution = solution + step_size * direction
        residual = residual - step_size * along_dir
        applied = operate(residual)
        norm_next, product = both_sums(residual, applied)
        beta_ratio = norm_next / norm_now
        step_next = norm_next / (product - beta_ratio * norm_next / step_size)
        direction = residual + beta_ratio * direction
        along_dir = applied + beta_ratio * along_dir
        return (solution, residual, direction, along_dir, norm_next, step_next)

    carry = (solution, residual, residual, applied, norm_now, step_size)
    solution, residual, direction, along_dir, norm_now, step_size = lax.fori_loop(
        0, ITERS - 1, iterate, carry
    )
    solution = solution + step_size * direction
    sol_pad = padded_2(solution, (("strip", 2),), 1)
    sol_pad = jnp.pad(sol_pad, ((0, 0), (0, 0), (0, 0), (1, 1)))
    forward_field = solution[:, 0]
    adjoint_field = solution[:, 1]
    fwd_pad = sol_pad[:, 0]
    adj_pad = sol_pad[:, 1]
    term_up = jnp.where(
        top_keep[None],
        (forward_field - fwd_pad[:, :-2, 1:-1]) * (adjoint_field - adj_pad[:, :-2, 1:-1]),
        0.0,
    )
    term_down = (forward_field - fwd_pad[:, 2:, 1:-1]) * (adjoint_field - adj_pad[:, 2:, 1:-1])
    term_left = (forward_field - fwd_pad[:, 1:-1, :-2]) * (adjoint_field - adj_pad[:, 1:-1, :-2])
    term_right = (forward_field - fwd_pad[:, 1:-1, 2:]) * (adjoint_field - adj_pad[:, 1:-1, 2:])
    partial_value = (wavenum * wavenum)[:, None, None] * forward_field * adjoint_field + 0.5 * (
        term_up + term_down + term_left + term_right
    )
    local_sum = jnp.sum(weights[:, None, None] * partial_value, axis=0)
    summed = lax.psum(local_sum, "wave")
    share_width = cell_count // lax.axis_size("wave")
    share_out = lax.dynamic_slice_in_dim(
        summed, lax.axis_index("wave") * share_width, share_width, 1
    )
    return -share_out


LANES = 128
PAD = 8
ROWS = 64
FIRST = 1
STEP = 256


def gathers_whole(shape, electrodes):
    waves, _, rows, cells = shape
    strips = lax.axis_size("strip")
    return (
        lax.axis_size("wave") == 2
        and rows * strips == ROWS
        and rows == PAD
        and strips >= waves + FIRST
        and cells == 2 * PAD * LANES
        and electrodes <= LANES
    )


def whole_kernel(
    nodes, pair, gains, scales, prior, sigma, out,
    fields, section, x, past, r, q, w, s, diag, up, down, left, charge, source, steps, grad, other, mine, parts,
    sigma_sent, sigma_got, field_sent, field_got, own_sem, core_sent, core_got, sent, got,
):
    strips = lax.axis_size("strip")
    strip = lax.axis_index("strip")
    core = lax.axis_index("wave")
    waves = prior.shape[0]
    depth = sigma.shape[0]
    half = q.shape[0]
    cells = 2 * half
    blocks = half // STEP
    here = pl.ds(pl.multiple_of(strip * depth, PAD), depth)
    peer = {"wave": 1 - core}
    mesh_id = pl.DeviceIdType.MESH
    solver = (strip >= FIRST) & (strip < FIRST + waves)

    barrier = pltpu.get_barrier_semaphore()
    for hop in range(1, strips):
        pl.semaphore_signal(
            barrier, inc=1, device_id={"strip": lax.rem(strip + hop, strips)}, device_id_type=mesh_id
        )
    pl.semaphore_signal(barrier, inc=1, device_id=peer, device_id_type=mesh_id)
    pl.semaphore_wait(barrier, strips)

    def remote(src, dst, send_sem, recv_sem, device):
        return pltpu.make_async_remote_copy(
            src_ref=src,
            dst_ref=dst,
            send_sem=send_sem,
            recv_sem=recv_sem,
            device_id=device,
            device_id_type=mesh_id,
        )

    my_side = pl.ds(pl.multiple_of(core * half, LANES), half)

    def sigma_copy(place):
        return remote(
            sigma.at[:, my_side],
            section.at[core, here, :],
            sigma_sent.at[place],
            sigma_got.at[strip],
            {"strip": place + FIRST},
        )

    def field_copy(place, c):
        return remote(
            prior.at[place, c],
            fields.at[c, here, :],
            field_sent.at[c, place],
            field_got.at[c, strip],
            {"strip": place + FIRST},
        )

    def own_sigma():
        return pltpu.make_async_copy(
            sigma.at[:, my_side], section.at[core, here, :], own_sem.at[2]
        )

    def own_field(c):
        return pltpu.make_async_copy(
            prior.at[strip - FIRST, c], fields.at[c, here, :], own_sem.at[c]
        )

    def each_other(body):
        for place in range(waves):

            @pl.when(strip != place + FIRST)
            def _(place=place):
                body(place)

    def from_others(body):
        for source in range(strips):

            @pl.when(strip != source)
            def _(source=source):
                body(source)

    def await_block(ref, sem):
        pltpu.make_async_copy(ref, ref, sem).wait()

    each_other(lambda place: sigma_copy(place).start())
    each_other(lambda place: field_copy(place, 0).start())
    @pl.when(solver)
    def _():
        own_sigma().start()
        own_field(0).start()
        own_field(1).start()

    def send_second():
        each_other(lambda place: sigma_copy(place).wait_send())
        each_other(lambda place: field_copy(place, 0).wait_send())
        each_other(lambda place: field_copy(place, 1).start())

    square = scales[0]
    weight = scales[1]
    lane = lax.broadcasted_iota(jnp.int32, (PAD, LANES), 1)
    second = lane >= ROWS
    band = lax.broadcasted_iota(jnp.int32, (PAD, LANES), 0)

    def swap(block):
        return pltpu.roll(block, ROWS, 1)

    def edges(ref):
        last = pltpu.roll(ref[pl.ds(half, PAD), :], 1, 0)
        ref[pl.ds(0, PAD), :] = jnp.where(
            band == 0, jnp.where(second, swap(last), 0.0), last
        )
        first = pltpu.roll(ref[pl.ds(PAD, PAD), :], PAD - 1, 0)
        ref[pl.ds(half + PAD, PAD), :] = jnp.where(
            band == PAD - 1, jnp.where(second, 0.0, swap(first)), first
        )

    def window(ref, block, shifts):
        tall = ref[pl.ds(block * STEP, STEP + (shifts - 1) * PAD), :]
        return [tall[shift * PAD : shift * PAD + STEP] for shift in range(shifts)]

    def turned(ref, read):
        for b in range(PAD):
            cols = pl.ds(b * LANES, LANES)
            more = pl.ds(half + b * LANES, LANES)
            both = jnp.concatenate([read(0, cols), read(1, more)], 0)
            ref[pl.ds(PAD + b, LANES, stride=PAD), :] = both.T

    def rows(block, shift=0):
        return pl.ds(block * STEP + shift, STEP)

    def fold(value):
        return jnp.sum(value.reshape(STEP // PAD, PAD, LANES), axis=0)

    def total(value):
        return jnp.sum(value, keepdims=True)

    def charges():
        line = lax.broadcasted_iota(jnp.int32, (1, LANES), 1)
        charge[...] = jnp.zeros_like(charge)

        def mark(e, spots):
            node = nodes[e]
            col = lax.rem(node, cells)
            side = lax.div(col, half)
            hit = line == side * ROWS + lax.div(node, cells)
            sign = jnp.where(pair[0] == e, 1.0, 0.0) - jnp.where(pair[1] == e, 1.0, 0.0)
            charge[0, pl.ds(e, 1), :] = jnp.where(hit, sign, 0.0)
            charge[1, pl.ds(e, 1), :] = jnp.where(hit, gains[e], 0.0)
            cell = lax.rem(col, half)
            spot = lax.rem(cell, LANES) * PAD + lax.div(cell, LANES)
            return jnp.where(line == e, spot, spots)

        return lax.fori_loop(0, nodes.shape[0], mark, jnp.full((1, LANES), -1, jnp.int32))

    def coefficients():
        row_lane = lax.rem(lax.broadcasted_iota(jnp.int32, (STEP, LANES), 1), ROWS)
        top = row_lane == 0
        bottom = row_lane == ROWS - 1
        turned(s, lambda side, cols: section[side, :, pl.ds(cols.start - side * half, LANES)])
        edges(s)
        for b in range(blocks):
            before, mid, after = window(s, b, 3)
            face_left = 0.5 * (mid + before)
            face_right = 0.5 * (mid + after)
            face_up = jnp.where(top, 0.0, 0.5 * (mid + pltpu.roll(mid, 1, 1)))
            below = jnp.where(bottom, 0.0, pltpu.roll(mid, LANES - 1, 1))
            face_down = 0.5 * (mid + below)
            up[rows(b), :] = face_up
            down[rows(b), :] = jnp.where(bottom, 0.0, face_down)
            left[rows(b), :] = face_left
            diag[rows(b), :] = face_up + face_down + face_left + face_right + square * mid
        tail = s[pl.ds(half + PAD, PAD), :]
        left[pl.ds(half, PAD), :] = 0.5 * (tail + s[pl.ds(half, PAD), :])

    def applied(ref, b):
        before, mid, after = window(ref, b, 3)
        face_left, face_right = window(left, b, 2)
        result = diag[rows(b), :] * mid - up[rows(b), :] * pltpu.roll(mid, 1, 1)
        result = result - down[rows(b), :] * pltpu.roll(mid, LANES - 1, 1)
        return mid, result - face_left * before - face_right * after

    def sources(spots):
        for c in range(2):
            for b in range(blocks):
                cell = b * STEP + lax.broadcasted_iota(jnp.int32, (STEP, LANES), 0)
                source[c, rows(b), :] = jnp.dot(
                    jnp.where(cell == spots, 1.0, 0.0),
                    charge[c],
                    precision=lax.Precision.HIGHEST,
                    preferred_element_type=jnp.float32,
                )

    def solve(c):
        xc = x.at[c]
        turned(xc, lambda _, cols: fields[c, :, cols])
        edges(xc)
        for b in range(blocks):
            value = source[c, rows(b), :] - applied(xc, b)[1]
            r[rows(b, PAD), :] = value
            past[0, rows(b), :] = value
        edges(r)

        def image(b, sums):
            mid, value = applied(r, b)
            w[rows(b), :] = value
            return sums[0] + fold(mid * mid), sums[1] + fold(mid * value)

        none = (jnp.zeros((PAD, LANES), jnp.float32),) * 2
        sums = none
        for b in range(blocks):
            sums = image(b, sums)
        norm, product = total(sums[0]), total(sums[1])
        size = norm / product
        for b in range(blocks):
            q[rows(b), :] = jnp.zeros((STEP, LANES), jnp.float32)

        def wide(value):
            return jnp.broadcast_to(value, (1, LANES))

        steps[0, pl.ds(0, 1), :] = wide(size)

        def iterate(k, carry):
            norm, size, ratio = carry
            per_norm, per_size = 1.0 / norm, 1.0 / size

            def advance(b):
                along = w[rows(b), :] + ratio * q[rows(b), :]
                q[rows(b), :] = along
                value = r[rows(b, PAD), :] - size * along
                r[rows(b, PAD), :] = value
                past[k + 1, rows(b), :] = value

            advance(blocks - 1)
            advance(0)
            edges(r)
            sums = none
            for b in range(blocks):
                if b + 1 < blocks - 1:
                    advance(b + 1)
                sums = image(b, sums)
            after, product = total(sums[0]), total(sums[1])
            ratio = after * per_norm
            size = after / (product - ratio * after * per_size)
            steps[0, pl.ds(k + 1, 1), :] = wide(size)
            steps[1, pl.ds(k + 1, 1), :] = wide(ratio)
            return after, size, ratio

        lax.fori_loop(0, ITERS - 1, iterate, (norm, size, jnp.zeros_like(norm)))
        gain = steps[0, pl.ds(ITERS - 1, 1), :]
        shares = [gain]
        for k in range(ITERS - 2, -1, -1):
            gain = steps[0, pl.ds(k, 1), :] + steps[1, pl.ds(k + 1, 1), :] * gain
            shares.insert(0, gain)
        for b in range(blocks):
            value = xc[rows(b, PAD), :]
            for k in range(ITERS):
                value = value + shares[k] * past[k, rows(b), :]
            xc[rows(b, PAD), :] = value
        edges(xc)

    core_swap = remote(section.at[core], section.at[core], core_sent.at[0], core_got.at[0], peer)
    grad_swap = remote(
        grad.at[pl.ds(pl.multiple_of((1 - core) * ROWS, ROWS), ROWS), :],
        other,
        core_sent.at[1],
        core_got.at[1],
        peer,
    )

    def part_copy(target):
        return remote(
            mine.at[pl.ds(target * depth, depth), :],
            parts.at[strip - FIRST],
            sent.at[target],
            got.at[strip - FIRST],
            {"strip": target},
        )

    @pl.when(jnp.logical_not(solver))
    def _():
        send_second()

    @pl.when(solver)
    def _():
        sources(charges())
        own_sigma().wait()
        from_others(
            lambda source: await_block(
                section.at[core, pl.ds(source * depth, depth), :], sigma_got.at[source]
            )
        )
        core_swap.start()
        core_swap.wait()
        send_second()
        coefficients()
        own_field(0).wait()
        from_others(
            lambda source: await_block(
                fields.at[0, pl.ds(source * depth, depth), :], field_got.at[0, source]
            )
        )
        solve(0)
        own_field(1).wait()
        from_others(
            lambda source: await_block(
                fields.at[1, pl.ds(source * depth, depth), :], field_got.at[1, source]
            )
        )
        solve(1)

        row_lane = lax.rem(lax.broadcasted_iota(jnp.int32, (STEP, LANES), 1), ROWS)
        for b in range(blocks):
            u_before, u, u_after = window(x.at[0], b, 3)
            v_before, v, v_after = window(x.at[1], b, 3)
            both = u * v
            term = (u - u_before) * (v - v_before)
            term = term + (u - u_after) * (v - v_after)
            rise = (u - pltpu.roll(u, 1, 1)) * (v - pltpu.roll(v, 1, 1))
            term = term + jnp.where(row_lane == 0, 0.0, rise)
            fall = pltpu.roll(rise, LANES - 1, 1)
            term = term + jnp.where(row_lane == ROWS - 1, both, fall)
            w[rows(b), :] = (-weight) * (square * both + 0.5 * term)
        for b in range(PAD):
            grad[:, pl.ds(b * LANES, LANES)] = w[pl.ds(b, LANES, stride=PAD), :].T

        grad_swap.start()
        grad_swap.wait_recv()
        mine[...] = grad[pl.ds(pl.multiple_of(core * ROWS, ROWS), ROWS), :] + other[...]
        for target in range(strips):

            @pl.when(strip != target)
            def _():
                part_copy(target).start()

        parts[strip - FIRST] = mine[here, :]

    for place in range(waves):

        @pl.when(strip != place + FIRST)
        def _():
            await_block(parts.at[place], got.at[place])

    result = parts[0]
    for place in range(1, waves):
        result = result + parts[place]
    out[...] = result

    each_other(lambda place: field_copy(place, 1).wait_send())

    @pl.when(solver)
    def _():
        grad_swap.wait_send()
        for target in range(strips):

            @pl.when(strip != target)
            def _():
                part_copy(target).wait_send()


def per_device_whole(prior_fields, conductivity, electrode_nodes, source_pair, innovation):
    waves, _, rows, cells = prior_fields.shape
    strips = lax.axis_size("strip")
    half = cells // 2
    padded = half + 2 * PAD
    vmem = pl.BlockSpec(memory_space=pltpu.VMEM)
    smem = pl.BlockSpec(memory_space=pltpu.SMEM)
    anywhere = pl.BlockSpec(memory_space=pltpu.HBM)
    f32 = jnp.float32
    dma = pltpu.SemaphoreType.DMA

    wave_id = lax.axis_index("wave") * waves + lax.axis_index("strip") - FIRST
    wavenum, weights = wave_table(wave_id.astype(f32))
    scales = jnp.stack([wavenum * wavenum, weights])
    return pl.pallas_call(
        whole_kernel,
        out_shape=jax.ShapeDtypeStruct((rows, half), f32),
        in_specs=[smem] * 4 + [anywhere] * 2,
        out_specs=vmem,
        scratch_shapes=[
            pltpu.VMEM((2, ROWS, cells), f32),
            pltpu.VMEM((2, ROWS, half), f32),
            pltpu.VMEM((2, padded, LANES), f32),
            pltpu.VMEM((ITERS, half, LANES), f32),
            pltpu.VMEM((padded, LANES), f32),
            pltpu.VMEM((half, LANES), f32),
            pltpu.VMEM((half, LANES), f32),
            pltpu.VMEM((padded, LANES), f32),
            pltpu.VMEM((half, LANES), f32),
            pltpu.VMEM((half, LANES), f32),
            pltpu.VMEM((half, LANES), f32),
            pltpu.VMEM((half + PAD, LANES), f32),
            pltpu.VMEM((2, LANES, LANES), f32),
            pltpu.VMEM((2, half, LANES), f32),
            pltpu.VMEM((2, 2 * PAD, LANES), f32),
            pltpu.VMEM((LANES, half), f32),
            pltpu.VMEM((ROWS, half), f32),
            pltpu.VMEM((ROWS, half), f32),
            pltpu.VMEM((waves, rows, half), f32),
            dma((waves,)),
            dma((strips,)),
            dma((2, waves)),
            dma((2, strips)),
            dma((3,)),
            dma((2,)),
            dma((2,)),
            dma((strips,)),
            dma((waves,)),
        ],
        compiler_params=pltpu.CompilerParams(
            collective_id=0, has_side_effects=True, vmem_limit_bytes=63 * 2**20
        ),
        name="solve_wave",
    )(electrode_nodes, source_pair, innovation, scales, prior_fields, conductivity)


def solution(mesh):
    in_specs = (
        P("wave", None, ("lines", "strip"), None),
        P(("lines", "strip"), None),
        P("lines"),
        P("lines"),
        P("lines"),
    )
    out_specs = P(("lines", "strip"), "wave")

    def per_device(prior_fields, *rest):
        if gathers_whole(prior_fields.shape, rest[-1].shape[0]):
            return per_device_whole(prior_fields, *rest)
        return per_device_strips(prior_fields, *rest)

    return jax.shard_map(
        per_device, mesh=mesh, in_specs=in_specs, out_specs=out_specs, check_vma=False
    )
```

```python
import math

import jax
import jax.numpy as jnp
from jax import lax
from jax.experimental import pallas as pl
from jax.experimental.pallas import tpu as pltpu
from jax.sharding import PartitionSpec as P

WAVES = 12
ITERS = 12


k_lowest = 0.01
k_highest = 1.0


def padded_2(block, sides, width):
    for axis, dim in sides:
        count = lax.axis_size(axis)
        forward = [(i, i + 1) for i in range(count - 1)]
        backward = [(target, source) for source, target in forward]
        low = lax.ppermute(
            lax.slice_in_dim(block, block.shape[dim] - width, None, axis=dim), axis, forward
        )
        high = lax.ppermute(lax.slice_in_dim(block, 0, width, axis=dim), axis, backward)
        block = jnp.concatenate([low, block, high], axis=dim)
    return block


def wave_table(position):
    spacing = (math.log(k_highest) - math.log(k_lowest)) / (WAVES - 1)
    wavenum = jnp.exp(math.log(k_lowest) + spacing * position)
    ends = jnp.where((position == 0) | (position == WAVES - 1), 0.5, 1.0)
    weights = 2.0 / math.pi * spacing * wavenum * ends
    return (wavenum, weights)


def inner_sums(first, second):
    return jnp.sum(first * second, axis=(2, 3), keepdims=True)


def per_device_strips(prior_fields, conductivity, electrode_nodes, source_pair, innovation):
    wave_dev = prior_fields.shape[0]
    row_count = prior_fields.shape[2]
    cell_count = prior_fields.shape[3]
    row_ids = lax.axis_index("strip") * row_count + jnp.arange(row_count, dtype=jnp.int32)
    top_keep = (row_ids != 0)[:, None]
    sig_pad = padded_2(conductivity, (("strip", 0),), 1)
    sig_pad = jnp.pad(sig_pad, ((0, 0), (1, 1)))
    face_up = jnp.where(top_keep, 0.5 * (conductivity + sig_pad[:-2, 1:-1]), 0.0)
    face_down = 0.5 * (conductivity + sig_pad[2:, 1:-1])
    face_left = 0.5 * (conductivity + sig_pad[1:-1, :-2])
    face_right = 0.5 * (conductivity + sig_pad[1:-1, 2:])
    wave_ids = (lax.axis_index("wave") * wave_dev + jnp.arange(wave_dev, dtype=jnp.int32)).astype(
        jnp.float32
    )
    wavenum, weights = wave_table(wave_ids)
    face_sum = face_up + face_down + face_left + face_right
    diagonal = (face_sum[None] + (wavenum * wavenum)[:, None, None] * conductivity[None])[:, None]

    def operate(vector):
        padded = padded_2(vector, (("strip", 2),), 1)
        padded = jnp.pad(padded, ((0, 0), (0, 0), (0, 0), (1, 1)))
        result = diagonal * vector - face_up * padded[:, :, :-2, 1:-1]
        result = result - face_down * padded[:, :, 2:, 1:-1]
        result = result - face_left * padded[:, :, 1:-1, :-2]
        return result - face_right * padded[:, :, 1:-1, 2:]

    electrode_ids = jnp.arange(innovation.shape[0], dtype=jnp.int32)
    forward = (electrode_ids == source_pair[0]).astype(jnp.float32) - (
        electrode_ids == source_pair[1]
    ).astype(jnp.float32)
    values = jnp.stack([forward, innovation])
    node_rows = electrode_nodes // cell_count
    node_cols = electrode_nodes % cell_count
    rows_hot = (node_rows[:, None] == row_ids[None, :]).astype(jnp.float32)
    cols_hot = (node_cols[:, None] == jnp.arange(cell_count, dtype=jnp.int32)[None, :]).astype(
        jnp.float32
    )
    weighted = values[:, :, None] * rows_hot[None]
    source = jnp.einsum("sez,ex->szx", weighted, cols_hot, precision=lax.Precision.HIGHEST)[None]
    solution = prior_fields
    residual = source - operate(solution)

    def both_sums(vector, applied):
        return lax.psum((inner_sums(vector, vector), inner_sums(vector, applied)), "strip")

    applied = operate(residual)
    norm_now, product = both_sums(residual, applied)
    step_size = norm_now / product

    def iterate(sweep, carry):
        solution, residual, direction, along_dir, norm_now, step_size = carry
        solution = solution + step_size * direction
        residual = residual - step_size * along_dir
        applied = operate(residual)
        norm_next, product = both_sums(residual, applied)
        beta_ratio = norm_next / norm_now
        step_next = norm_next / (product - beta_ratio * norm_next / step_size)
        direction = residual + beta_ratio * direction
        along_dir = applied + beta_ratio * along_dir
        return (solution, residual, direction, along_dir, norm_next, step_next)

    carry = (solution, residual, residual, applied, norm_now, step_size)
    solution, residual, direction, along_dir, norm_now, step_size = lax.fori_loop(
        0, ITERS - 1, iterate, carry
    )
    solution = solution + step_size * direction
    sol_pad = padded_2(solution, (("strip", 2),), 1)
    sol_pad = jnp.pad(sol_pad, ((0, 0), (0, 0), (0, 0), (1, 1)))
    forward_field = solution[:, 0]
    adjoint_field = solution[:, 1]
    fwd_pad = sol_pad[:, 0]
    adj_pad = sol_pad[:, 1]
    term_up = jnp.where(
        top_keep[None],
        (forward_field - fwd_pad[:, :-2, 1:-1]) * (adjoint_field - adj_pad[:, :-2, 1:-1]),
        0.0,
    )
    term_down = (forward_field - fwd_pad[:, 2:, 1:-1]) * (adjoint_field - adj_pad[:, 2:, 1:-1])
    term_left = (forward_field - fwd_pad[:, 1:-1, :-2]) * (adjoint_field - adj_pad[:, 1:-1, :-2])
    term_right = (forward_field - fwd_pad[:, 1:-1, 2:]) * (adjoint_field - adj_pad[:, 1:-1, 2:])
    partial_value = (wavenum * wavenum)[:, None, None] * forward_field * adjoint_field + 0.5 * (
        term_up + term_down + term_left + term_right
    )
    local_sum = jnp.sum(weights[:, None, None] * partial_value, axis=0)
    summed = lax.psum(local_sum, "wave")
    share_width = cell_count // lax.axis_size("wave")
    share_out = lax.dynamic_slice_in_dim(
        summed, lax.axis_index("wave") * share_width, share_width, 1
    )
    return -share_out


LANES = 128
PAD = 8
ROWS = 64
FIRST = 1
STEP = 512


def gathers_whole(shape, electrodes):
    waves, _, rows, cells = shape
    strips = lax.axis_size("strip")
    return (
        lax.axis_size("wave") == 2
        and rows * strips == ROWS
        and rows == PAD
        and strips >= waves + FIRST
        and cells == 2 * PAD * LANES
        and electrodes <= LANES
    )


def whole_kernel(
    nodes, pair, gains, scales, prior, sigma, out,
    fields, section, x, past, r, q, w, s, diag, up, down, left, charge, source, steps, grad, other, mine, parts,
    sigma_sent, sigma_got, field_sent, field_got, own_sem, core_sent, core_got, sent, got,
):
    strips = lax.axis_size("strip")
    strip = lax.axis_index("strip")
    core = lax.axis_index("wave")
    waves = prior.shape[0]
    depth = sigma.shape[0]
    half = q.shape[0]
    cells = 2 * half
    blocks = half // STEP
    here = pl.ds(pl.multiple_of(strip * depth, PAD), depth)
    peer = {"wave": 1 - core}
    mesh_id = pl.DeviceIdType.MESH
    solver = (strip >= FIRST) & (strip < FIRST + waves)

    barrier = pltpu.get_barrier_semaphore()
    for hop in range(1, strips):
        pl.semaphore_signal(
            barrier, inc=1, device_id={"strip": lax.rem(strip + hop, strips)}, device_id_type=mesh_id
        )
    pl.semaphore_signal(barrier, inc=1, device_id=peer, device_id_type=mesh_id)
    pl.semaphore_wait(barrier, strips)

    def remote(src, dst, send_sem, recv_sem, device):
        return pltpu.make_async_remote_copy(
            src_ref=src,
            dst_ref=dst,
            send_sem=send_sem,
            recv_sem=recv_sem,
            device_id=device,
            device_id_type=mesh_id,
        )

    my_side = pl.ds(pl.multiple_of(core * half, LANES), half)

    def sigma_copy(place):
        return remote(
            sigma.at[:, my_side],
            section.at[core, here, :],
            sigma_sent.at[place],
            sigma_got.at[strip],
            {"strip": place + FIRST},
        )

    def field_copy(place, c):
        return remote(
            prior.at[place, c],
            fields.at[c, here, :],
            field_sent.at[c, place],
            field_got.at[c, strip],
            {"strip": place + FIRST},
        )

    def own_sigma():
        return pltpu.make_async_copy(
            sigma.at[:, my_side], section.at[core, here, :], own_sem.at[2]
        )

    def own_field(c):
        return pltpu.make_async_copy(
            prior.at[strip - FIRST, c], fields.at[c, here, :], own_sem.at[c]
        )

    def each_other(body):
        for turn in range(waves):
            place = lax.rem(strip + turn, waves)

            @pl.when(strip != place + FIRST)
            def _(place=place):
                body(place)

    def from_others(body):
        for source in range(strips):

            @pl.when(strip != source)
            def _(source=source):
                body(source)

    def await_block(ref, sem):
        pltpu.make_async_copy(ref, ref, sem).wait()

    each_other(lambda place: sigma_copy(place).start())
    each_other(lambda place: field_copy(place, 0).start())
    @pl.when(solver)
    def _():
        own_sigma().start()
        own_field(0).start()
        own_field(1).start()

    def send_second():
        each_other(lambda place: sigma_copy(place).wait_send())
        each_other(lambda place: field_copy(place, 0).wait_send())
        each_other(lambda place: field_copy(place, 1).start())

    square = scales[0]
    weight = scales[1]
    lane = lax.broadcasted_iota(jnp.int32, (PAD, LANES), 1)
    second = lane >= ROWS
    band = lax.broadcasted_iota(jnp.int32, (PAD, LANES), 0)

    def swap(block):
        return pltpu.roll(block, ROWS, 1)

    def edges(ref):
        last = pltpu.roll(ref[pl.ds(half, PAD), :], 1, 0)
        ref[pl.ds(0, PAD), :] = jnp.where(
            band == 0, jnp.where(second, swap(last), 0.0), last
        )
        first = pltpu.roll(ref[pl.ds(PAD, PAD), :], PAD - 1, 0)
        ref[pl.ds(half + PAD, PAD), :] = jnp.where(
            band == PAD - 1, jnp.where(second, 0.0, swap(first)), first
        )

    def window(ref, block, shifts):
        tall = ref[pl.ds(block * STEP, STEP + (shifts - 1) * PAD), :]
        return [tall[shift * PAD : shift * PAD + STEP] for shift in range(shifts)]

    def turned(ref, read):
        for b in range(PAD):
            cols = pl.ds(b * LANES, LANES)
            more = pl.ds(half + b * LANES, LANES)
            both = jnp.concatenate([read(0, cols), read(1, more)], 0)
            ref[pl.ds(PAD + b, LANES, stride=PAD), :] = both.T

    def rows(block, shift=0):
        return pl.ds(block * STEP + shift, STEP)

    def fold(value):
        return jnp.sum(value.reshape(STEP // PAD, PAD, LANES), axis=0)

    def total(value):
        return jnp.sum(value, keepdims=True)

    def charges():
        line = lax.broadcasted_iota(jnp.int32, (1, LANES), 1)
        charge[...] = jnp.zeros_like(charge)

        def mark(e, spots):
            node = nodes[e]
            col = lax.rem(node, cells)
            side = lax.div(col, half)
            hit = line == side * ROWS + lax.div(node, cells)
            sign = jnp.where(pair[0] == e, 1.0, 0.0) - jnp.where(pair[1] == e, 1.0, 0.0)
            charge[0, pl.ds(e, 1), :] = jnp.where(hit, sign, 0.0)
            charge[1, pl.ds(e, 1), :] = jnp.where(hit, gains[e], 0.0)
            cell = lax.rem(col, half)
            spot = lax.rem(cell, LANES) * PAD + lax.div(cell, LANES)
            return jnp.where(line == e, spot, spots)

        return lax.fori_loop(0, nodes.shape[0], mark, jnp.full((1, LANES), -1, jnp.int32))

    def coefficients():
        row_lane = lax.rem(lax.broadcasted_iota(jnp.int32, (STEP, LANES), 1), ROWS)
        top = row_lane == 0
        bottom = row_lane == ROWS - 1
        turned(s, lambda side, cols: section[side, :, pl.ds(cols.start - side * half, LANES)])
        edges(s)
        for b in range(blocks):
            before, mid, after = window(s, b, 3)
            face_left = 0.5 * (mid + before)
            face_right = 0.5 * (mid + after)
            face_up = jnp.where(top, 0.0, 0.5 * (mid + pltpu.roll(mid, 1, 1)))
            below = jnp.where(bottom, 0.0, pltpu.roll(mid, LANES - 1, 1))
            face_down = 0.5 * (mid + below)
            up[rows(b), :] = face_up
            down[rows(b), :] = jnp.where(bottom, 0.0, face_down)
            left[rows(b), :] = face_left
            diag[rows(b), :] = face_up + face_down + face_left + face_right + square * mid
        tail = s[pl.ds(half + PAD, PAD), :]
        left[pl.ds(half, PAD), :] = 0.5 * (tail + s[pl.ds(half, PAD), :])

    def applied(ref, b):
        before, mid, after = window(ref, b, 3)
        face_left, face_right = window(left, b, 2)
        result = diag[rows(b), :] * mid - up[rows(b), :] * pltpu.roll(mid, 1, 1)
        result = result - down[rows(b), :] * pltpu.roll(mid, LANES - 1, 1)
        return mid, result - face_left * before - face_right * after

    def sources(spots):
        for c in range(2):
            for b in range(blocks):
                cell = b * STEP + lax.broadcasted_iota(jnp.int32, (STEP, LANES), 0)
                source[c, rows(b), :] = jnp.dot(
                    jnp.where(cell == spots, 1.0, 0.0),
                    charge[c],
                    precision=lax.Precision.HIGHEST,
                    preferred_element_type=jnp.float32,
                )

    def solve(c):
        xc = x.at[c]
        turned(xc, lambda _, cols: fields[c, :, cols])
        edges(xc)
        for b in range(blocks):
            value = source[c, rows(b), :] - applied(xc, b)[1]
            r[rows(b, PAD), :] = value
            past[0, rows(b), :] = value
        edges(r)

        def image(b, sums):
            mid, value = applied(r, b)
            w[rows(b), :] = value
            return sums[0] + fold(mid * mid), sums[1] + fold(mid * value)

        none = (jnp.zeros((PAD, LANES), jnp.float32),) * 2
        sums = none
        for b in range(blocks):
            sums = image(b, sums)
        norm, product = total(sums[0]), total(sums[1])
        size = norm / product
        for b in range(blocks):
            q[rows(b), :] = jnp.zeros((STEP, LANES), jnp.float32)

        def wide(value):
            return jnp.broadcast_to(value, (1, LANES))

        steps[0, pl.ds(0, 1), :] = wide(size)

        def iterate(k, carry):
            norm, size, ratio = carry
            per_norm, per_size = 1.0 / norm, 1.0 / size

            def advance(b):
                along = w[rows(b), :] + ratio * q[rows(b), :]
                q[rows(b), :] = along
                value = r[rows(b, PAD), :] - size * along
                r[rows(b, PAD), :] = value
                past[k + 1, rows(b), :] = value

            advance(blocks - 1)
            advance(0)
            edges(r)
            sums = none
            for b in range(blocks):
                if b + 1 < blocks - 1:
                    advance(b + 1)
                sums = image(b, sums)
            after, product = total(sums[0]), total(sums[1])
            ratio = after * per_norm
            size = after / (product - ratio * after * per_size)
            steps[0, pl.ds(k + 1, 1), :] = wide(size)
            steps[1, pl.ds(k + 1, 1), :] = wide(ratio)
            return after, size, ratio

        lax.fori_loop(0, ITERS - 1, iterate, (norm, size, jnp.zeros_like(norm)))
        gain = steps[0, pl.ds(ITERS - 1, 1), :]
        shares = [gain]
        for k in range(ITERS - 2, -1, -1):
            gain = steps[0, pl.ds(k, 1), :] + steps[1, pl.ds(k + 1, 1), :] * gain
            shares.insert(0, gain)
        for b in range(blocks):
            value = xc[rows(b, PAD), :]
            for k in range(ITERS):
                value = value + shares[k] * past[k, rows(b), :]
            xc[rows(b, PAD), :] = value
        edges(xc)

    core_swap = remote(section.at[core], section.at[core], core_sent.at[0], core_got.at[0], peer)
    grad_swap = remote(
        grad.at[pl.ds(pl.multiple_of((1 - core) * ROWS, ROWS), ROWS), :],
        other,
        core_sent.at[1],
        core_got.at[1],
        peer,
    )

    def part_copy(target):
        return remote(
            mine.at[pl.ds(pl.multiple_of(target * depth, PAD), depth), :],
            parts.at[strip - FIRST],
            sent.at[target],
            got.at[strip - FIRST],
            {"strip": target},
        )

    @pl.when(jnp.logical_not(solver))
    def _():
        send_second()

    @pl.when(solver)
    def _():
        sources(charges())
        own_sigma().wait()
        from_others(
            lambda source: await_block(
                section.at[core, pl.ds(source * depth, depth), :], sigma_got.at[source]
            )
        )
        core_swap.start()
        core_swap.wait()
        send_second()
        coefficients()
        own_field(0).wait()
        from_others(
            lambda source: await_block(
                fields.at[0, pl.ds(source * depth, depth), :], field_got.at[0, source]
            )
        )
        solve(0)
        own_field(1).wait()
        from_others(
            lambda source: await_block(
                fields.at[1, pl.ds(source * depth, depth), :], field_got.at[1, source]
            )
        )
        solve(1)

        row_lane = lax.rem(lax.broadcasted_iota(jnp.int32, (STEP, LANES), 1), ROWS)
        for b in range(blocks):
            u_before, u, u_after = window(x.at[0], b, 3)
            v_before, v, v_after = window(x.at[1], b, 3)
            both = u * v
            term = (u - u_before) * (v - v_before)
            term = term + (u - u_after) * (v - v_after)
            rise = (u - pltpu.roll(u, 1, 1)) * (v - pltpu.roll(v, 1, 1))
            term = term + jnp.where(row_lane == 0, 0.0, rise)
            fall = pltpu.roll(rise, LANES - 1, 1)
            term = term + jnp.where(row_lane == ROWS - 1, both, fall)
            w[rows(b), :] = (-weight) * (square * both + 0.5 * term)
        for b in range(PAD):
            grad[:, pl.ds(b * LANES, LANES)] = w[pl.ds(b, LANES, stride=PAD), :].T

        grad_swap.start()
        grad_swap.wait_recv()
        mine[...] = grad[pl.ds(pl.multiple_of(core * ROWS, ROWS), ROWS), :] + other[...]
        for hop in range(1, strips):
            part_copy(lax.rem(strip + hop, strips)).start()

        parts[strip - FIRST] = mine[here, :]

    for place in range(waves):

        @pl.when(strip != place + FIRST)
        def _():
            await_block(parts.at[place], got.at[place])

    result = parts[0]
    for place in range(1, waves):
        result = result + parts[place]
    out[...] = result

    each_other(lambda place: field_copy(place, 1).wait_send())

    @pl.when(solver)
    def _():
        grad_swap.wait_send()
        for target in range(strips):

            @pl.when(strip != target)
            def _():
                part_copy(target).wait_send()


def per_device_whole(prior_fields, conductivity, electrode_nodes, source_pair, innovation):
    waves, _, rows, cells = prior_fields.shape
    strips = lax.axis_size("strip")
    half = cells // 2
    padded = half + 2 * PAD
    vmem = pl.BlockSpec(memory_space=pltpu.VMEM)
    smem = pl.BlockSpec(memory_space=pltpu.SMEM)
    anywhere = pl.BlockSpec(memory_space=pltpu.HBM)
    f32 = jnp.float32
    dma = pltpu.SemaphoreType.DMA

    wave_id = lax.axis_index("wave") * waves + lax.axis_index("strip") - FIRST
    wavenum, weights = wave_table(wave_id.astype(f32))
    scales = jnp.stack([wavenum * wavenum, weights])
    return pl.pallas_call(
        whole_kernel,
        out_shape=jax.ShapeDtypeStruct((rows, half), f32),
        in_specs=[smem] * 4 + [anywhere] * 2,
        out_specs=vmem,
        scratch_shapes=[
            pltpu.VMEM((2, ROWS, cells), f32),
            pltpu.VMEM((2, ROWS, half), f32),
            pltpu.VMEM((2, padded, LANES), f32),
            pltpu.VMEM((ITERS, half, LANES), f32),
            pltpu.VMEM((padded, LANES), f32),
            pltpu.VMEM((half, LANES), f32),
            pltpu.VMEM((half, LANES), f32),
            pltpu.VMEM((padded, LANES), f32),
            pltpu.VMEM((half, LANES), f32),
            pltpu.VMEM((half, LANES), f32),
            pltpu.VMEM((half, LANES), f32),
            pltpu.VMEM((half + PAD, LANES), f32),
            pltpu.VMEM((2, LANES, LANES), f32),
            pltpu.VMEM((2, half, LANES), f32),
            pltpu.VMEM((2, 2 * PAD, LANES), f32),
            pltpu.VMEM((LANES, half), f32),
            pltpu.VMEM((ROWS, half), f32),
            pltpu.VMEM((ROWS, half), f32),
            pltpu.VMEM((waves, rows, half), f32),
            dma((waves,)),
            dma((strips,)),
            dma((2, waves)),
            dma((2, strips)),
            dma((3,)),
            dma((2,)),
            dma((2,)),
            dma((strips,)),
            dma((waves,)),
        ],
        compiler_params=pltpu.CompilerParams(
            collective_id=0, has_side_effects=True, vmem_limit_bytes=63 * 2**20
        ),
        name="solve_wave",
    )(electrode_nodes, source_pair, innovation, scales, prior_fields, conductivity)


def solution(mesh):
    in_specs = (
        P("wave", None, ("lines", "strip"), None),
        P(("lines", "strip"), None),
        P("lines"),
        P("lines"),
        P("lines"),
    )
    out_specs = P(("lines", "strip"), "wave")

    def per_device(prior_fields, *rest):
        if gathers_whole(prior_fields.shape, rest[-1].shape[0]):
            return per_device_whole(prior_fields, *rest)
        return per_device_strips(prior_fields, *rest)

    return jax.shard_map(
        per_device, mesh=mesh, in_specs=in_specs, out_specs=out_specs, check_vma=False
    )
```
